32 devices in a mesh: dom: 2 (over y), col: 4 (over z), row: 2 (over x), sub: 2 (over core).
Axes of the slice: x: 2, y: 2, z: 4, core: 2. Of those that a mesh axis runs over, the one named last changes fastest.
Arguments:
- blocks: float32 [8, 4, 16, 256, 256], P(('dom', 'row', 'sub'), 'col'), parts along dimension 0, may hold values from -6 to 6
- block_slot: int32 [8, 4, 16], P(('dom', 'row', 'sub'), 'col'), parts along dimension 0, may hold values from 0 to 31, as said below
- basis_in: float32 [16, 16384], P(None, ('dom', 'col', 'row', 'sub')), parts along dimension 1, may hold values from -6 to 6
Outputs:
- basis_out: float32 [16, 16384], P(None, ('dom', 'col', 'row', 'sub')), parts along dimension 1
- factor: float32 [32, 16], P('dom'), parts along dimension 0
The draws below stay inside these ranges and needn't reach their ends.
There are 2 independent parts, one for each index of `dom`. The reference program is written for one: setup_inputs(seed, part) draws one part's arguments, and reference() takes and returns one part's arrays. A program takes and returns all parts, laid end to end along the dimension named above; each array names one. Nothing has to cross between parts.
Inputs may be any that keep to these rules, and one draw needn't show every extreme that they name: `block_slot`: within one device's 16 entries all slots differ; every device holds slot 0 and slot 31.
All inputs are finite; a program needn't handle non-finite values.
Results may differ from the reference program's by a relative error of at most 0.0003.
Values sent between devices are 32-bit elements; how exact they have to be, the bound alone decides.
No kernel may reach another device: no remote copies, remote signals or barrier semaphores. Data moves between devices by JAX's collectives and lax.ppermute only.
A program may use at most 64 MiB of HBM per device.

```python
import jax
import jax.numpy as jnp
from jax import lax

BLOCK_EDGE = 256
VECTOR_COUNT = 16
RBL = 4
COLUMN_BLOCKS = 8
NBLK = 16
RGROUPS = 4
CSHARDS = 4
NCOL = 8192


def draw_block_slot(key, part):
    key = jax.random.fold_in(key, 7)
    keys = jax.random.split(key, RGROUPS * CSHARDS)
    total = RBL * COLUMN_BLOCKS

    def one_device(single):
        inner = jax.random.permutation(single, total - 2)[:NBLK - 2] + 1
        ends = jnp.array([0, total - 1], dtype=jnp.int32)
        return jnp.concatenate([ends, inner.astype(jnp.int32)])
    slots = jax.vmap(one_device)(keys)
    return slots.reshape(RGROUPS, CSHARDS, NBLK).astype(jnp.int32)


def steps_of(key, shape, cuts, least, high):
    def one(position, blocks):
        steps = jax.random.uniform(jax.random.fold_in(jax.random.fold_in(key, 6), position), (blocks,), jnp.float32, least / len(cuts), high / len(cuts))
        return jnp.repeat(jnp.exp(steps), shape[position] // blocks).reshape((-1,) + (1,) * (len(shape) - position - 1))

    factor_of = one(*cuts[0])
    for cut in cuts[1:]:
        factor_of = factor_of * one(*cut)
    return factor_of


def noise(key, dims, deviation, bound, pieces=(), kind=jnp.bfloat16):
    entries = deviation * jax.random.normal(key, dims, jnp.float32)
    if pieces:
        entries = entries * steps_of(key, dims, pieces, -0.22, 0.18)
    return jnp.clip(entries, -bound, bound).astype(kind)


def setup_inputs(seed: int = 0, part: int = 0) -> dict:
    splits = jax.random.split(jax.random.key(seed), 4)
    own_keys = jax.random.split(jax.random.fold_in(splits[3], part), 4)
    return {
        "blocks": noise(own_keys[0], (RGROUPS, CSHARDS, NBLK, BLOCK_EDGE, BLOCK_EDGE), 1.0, 6.0, ((0, 4), (1, 4)), jnp.float32),
        "block_slot": draw_block_slot(jax.random.fold_in(jax.random.fold_in(splits[3], part), 71), part),
        "basis_in": noise(own_keys[2], (VECTOR_COUNT, NCOL), 1.0, 6.0, ((1, 16),), jnp.float32),
    }


PRECISION_LEVEL = lax.Precision.HIGHEST

def one_hots(slot):
    rowb = slot // COLUMN_BLOCKS
    colb = slot % COLUMN_BLOCKS
    row_hot = (rowb[:, None] == jnp.arange(RBL, dtype=jnp.int32)[None, :]).astype(jnp.float32)
    column_onehot = (colb[:, None] == jnp.arange(COLUMN_BLOCKS, dtype=jnp.int32)[None, :]).astype(jnp.float32)
    return (row_hot, column_onehot)

def local_rows(stored_block, slot, vector_column):
    row_hot, column_onehot = one_hots(slot)
    vector_select = jnp.einsum('fte,rt->fre', vector_column.reshape(VECTOR_COUNT, COLUMN_BLOCKS, BLOCK_EDGE), column_onehot, precision=PRECISION_LEVEL)
    block_product = jnp.einsum('dvc,vyc->dvy', vector_select, stored_block, precision=PRECISION_LEVEL)
    return jnp.einsum('kbi,br->kri', block_product, row_hot, precision=PRECISION_LEVEL).reshape(VECTOR_COUNT, RBL * BLOCK_EDGE)

def local_cols(stored_block, slot, yrow):
    row_hot, column_onehot = one_hots(slot)
    ysel = jnp.einsum('kri,br->kbi', yrow.reshape(VECTOR_COUNT, RBL, BLOCK_EDGE), row_hot, precision=PRECISION_LEVEL)
    block_product = jnp.einsum('kbi,bij->kbj', ysel, stored_block, precision=PRECISION_LEVEL)
    return jnp.einsum('kbj,bc->kcj', block_product, column_onehot, precision=PRECISION_LEVEL).reshape(VECTOR_COUNT, COLUMN_BLOCKS * BLOCK_EDGE)

def reference(blocks, block_slot, basis_in):
    vsh = basis_in.reshape(VECTOR_COUNT, CSHARDS, COLUMN_BLOCKS * BLOCK_EDGE)

    def row_group(pair):
        blk_g, slot_g = pair
        parts = jax.vmap(local_rows, in_axes=(0, 0, 1))(blk_g, slot_g, vsh)
        yrow = lax.optimization_barrier(jnp.sum(parts, axis=0))
        return jax.vmap(local_cols, in_axes=(0, 0, None))(blk_g, slot_g, yrow)
    zparts = lax.map(row_group, (blocks, block_slot))
    zsum = lax.optimization_barrier(jnp.sum(zparts, axis=0))
    zmat = jnp.transpose(zsum, (1, 0, 2)).reshape(VECTOR_COUNT, NCOL)
    gram = jnp.dot(zmat, zmat.T, precision=PRECISION_LEVEL)
    lower = jnp.linalg.cholesky(gram)
    solved = lax.linalg.triangular_solve(lower, zmat, left_side=True, lower=True)
    basis_out = solved * jnp.sqrt(jnp.float32(NCOL))
    return (basis_out, lower.T)
```

```python
import math

import jax
import jax.numpy as jnp
from jax import lax
from jax.experimental import pallas as pl
from jax.experimental.pallas import tpu as pltpu
from jax.sharding import PartitionSpec as P

RBL = 4
GROUP = ("row", "sub")
VMEM_LIMIT = 24 * 1024 * 1024

NT = (((1,), (1,)), ((), ()))
NN = (((1,), (0,)), ((), ()))


def params():
    return pltpu.CompilerParams(vmem_limit_bytes=VMEM_LIMIT)


def vmem():
    return pl.BlockSpec(memory_space=pltpu.VMEM)


def smem():
    return pl.BlockSpec(memory_space=pltpu.SMEM)


def halves(x):
    high = x.astype(jnp.bfloat16)
    low = (x - high.astype(jnp.float32)).astype(jnp.bfloat16)
    return high, low


def split_kernel(blocks_ref, high_ref, low_ref):
    for i in range(blocks_ref.shape[0]):
        high_ref[i], low_ref[i] = halves(blocks_ref[i])


def split_blocks(blocks):
    n, rows, cols = blocks.shape
    return pl.pallas_call(
        split_kernel,
        out_shape=(
            pltpu.VMEM(blocks.shape, jnp.bfloat16),
            pltpu.VMEM(blocks.shape, jnp.bfloat16),
        ),
        in_specs=[vmem()],
        out_specs=(vmem(), vmem()),
        compiler_params=params(),
        cost_estimate=pl.CostEstimate(flops=3 * n * rows * cols, bytes_accessed=8 * n * rows * cols, transcendentals=0),
    )(blocks)


def store_halves(ref, index, x):
    count = x.shape[0]
    high, low = halves(x)
    ref[index, pl.ds(0, count)] = high
    ref[index, pl.ds(count, count)] = low


def product(pair, high, low, dims):
    count = pair.shape[0] // 2
    first = lax.dot_general(pair, high, dims, preferred_element_type=jnp.float32)
    second = lax.dot_general(pair[:count], low, dims, preferred_element_type=jnp.float32)
    return first[:count] + first[count:] + second


def rows_kernel(slot_ref, high_ref, low_ref, *refs):
    pieces, out_ref, pair_ref = refs[:-2], refs[-2], refs[-1]
    nblk, edge = high_ref.shape[0], high_ref.shape[1]
    per_piece = pieces[0].shape[1] // edge
    column_count = per_piece * len(pieces)
    me = lax.axis_index(GROUP)
    for k, piece in enumerate(pieces):
        for h in range(per_piece):
            store_halves(pair_ref, (me ^ k) * per_piece + h, piece[:, h * edge:(h + 1) * edge])
    out_ref[...] = jnp.zeros_like(out_ref)
    for b in range(nblk):
        slot = slot_ref[b]
        r, c = slot // column_count, slot % column_count
        out_ref[r] += product(pair_ref[c], high_ref[b], low_ref[b], NT)


def rows_product(slot, high, low, pieces):
    count = pieces[0].shape[0]
    nblk, edge = high.shape[0], high.shape[1]
    column_count = len(pieces) * pieces[0].shape[1] // edge
    return pl.pallas_call(
        rows_kernel,
        out_shape=jax.ShapeDtypeStruct((RBL, count, edge), jnp.float32),
        in_specs=[smem()] + [vmem()] * (2 + len(pieces)),
        out_specs=vmem(),
        scratch_shapes=[pltpu.VMEM((column_count, 2 * count, edge), jnp.bfloat16)],
        compiler_params=params(),
    )(slot, high, low, *pieces)


def cols_kernel(column_count, slot_ref, high_ref, low_ref, *refs):
    pieces, out_ref, pair_ref = refs[:-2], refs[-2], refs[-1]
    nblk = high_ref.shape[0]
    for r in range(RBL):
        total = pieces[0][r]
        for piece in pieces[1:]:
            total = total + piece[r]
        store_halves(pair_ref, r, total)
    out_ref[...] = jnp.zeros_like(out_ref)
    for b in range(nblk):
        slot = slot_ref[b]
        r, c = slot // column_count, slot % column_count
        out_ref[c] += product(pair_ref[r], high_ref[b], low_ref[b], NN)


def cols_product(slot, high, low, pieces, column_count):
    _, count, edge = pieces[0].shape
    return pl.pallas_call(
        lambda *refs: cols_kernel(column_count, *refs),
        out_shape=jax.ShapeDtypeStruct((column_count, count, edge), jnp.float32),
        in_specs=[smem()] + [vmem()] * (2 + len(pieces)),
        out_specs=vmem(),
        scratch_shapes=[pltpu.VMEM((RBL, 2 * count, edge), jnp.bfloat16)],
        compiler_params=params(),
    )(slot, high, low, *pieces)


def gram_kernel(a_ref, b_ref, z_ref, gram_ref):
    total = None
    for c in range(a_ref.shape[0]):
        z = a_ref[c] + b_ref[c]
        z_ref[c] = z
        g = lax.dot_general(z, z, NT, precision=lax.Precision.HIGHEST, preferred_element_type=jnp.float32)
        total = g if total is None else total + g
    gram_ref[...] = total


def gram_of(a, b):
    count = a.shape[1]
    return pl.pallas_call(
        gram_kernel,
        out_shape=(
            jax.ShapeDtypeStruct(a.shape, jnp.float32),
            jax.ShapeDtypeStruct((count, count), jnp.float32),
        ),
        in_specs=[vmem(), vmem()],
        out_specs=(vmem(), vmem()),
        compiler_params=params(),
    )(a, b)


def solve_kernel(scale, z_ref, *refs):
    grams, out_ref, factor_ref = refs[:-2], refs[-2], refs[-1]
    count = factor_ref.shape[0]
    per_share = out_ref.shape[1] // z_ref.shape[2]
    first = lax.axis_index(GROUP) * per_share
    g = grams[0][...]
    for piece in grams[1:]:
        g = g + piece[...]
    z = [z_ref[first + h] * scale for h in range(per_share)]
    row_id = lax.broadcasted_iota(jnp.int32, (count, count), 0)
    col_id = lax.broadcasted_iota(jnp.int32, (count, count), 1)
    factor = jnp.zeros((count, count), jnp.float32)
    edge = z_ref.shape[2]
    row_wide = lax.broadcasted_iota(jnp.int32, (count, edge), 0)
    done = [jnp.zeros_like(x) for x in z]
    for j in range(count):
        inverse = lax.rsqrt(g[j:j + 1, j:j + 1])
        row = g[j:j + 1, :] * inverse
        column = g[:, j:j + 1] * inverse
        factor = jnp.where((row_id == j) & (col_id >= j), row, factor)
        rows = [x[j:j + 1, :] * inverse for x in z]
        done = [jnp.where(row_wide == j, x, d) for x, d in zip(rows, done)]
        if j + 1 < count:
            g = g - column * row
            z = [x - column * y for x, y in zip(z, rows)]
    for h in range(per_share):
        out_ref[:, h * edge:(h + 1) * edge] = done[h]
    factor_ref[...] = factor


def solve(z, grams, share, scale):
    count = z.shape[1]
    return pl.pallas_call(
        lambda *refs: solve_kernel(scale, *refs),
        out_shape=(
            jax.ShapeDtypeStruct((count, share), jnp.float32),
            jax.ShapeDtypeStruct((count, count), jnp.float32),
        ),
        in_specs=[vmem()] * (1 + len(grams)),
        out_specs=(vmem(), vmem()),
        compiler_params=params(),
    )(z, *grams)


def partner(x, axes, k):
    n = lax.axis_size(axes)
    return lax.ppermute(x, axes, [(i, i ^ k) for i in range(n)])


def is_power(n):
    return n & (n - 1) == 0


def gather(x, axes):
    n = lax.axis_size(axes)
    return [x] + [partner(x, axes, k) for k in range(1, n)]


def to_sum(x, axis):
    n = lax.axis_size(axis)
    if n <= 4 and is_power(n):
        return gather(x, axis)
    return [lax.psum(x, axis)]


def body(blocks, block_slot, basis_in):
    edge = blocks.shape[-1]
    nblk = blocks.shape[2]
    share = basis_in.shape[1]
    column_count = share * lax.axis_size(GROUP) // edge
    slot = block_slot.reshape(nblk)
    high, low = split_blocks(blocks.reshape(nblk, edge, edge))
    high = pltpu.with_memory_space_constraint(high, pltpu.VMEM)
    low = pltpu.with_memory_space_constraint(low, pltpu.VMEM)
    ypart = rows_product(slot, high, low, gather(basis_in, GROUP))
    zpart = cols_product(slot, high, low, to_sum(ypart, "col"), column_count)
    rounds = [(axis, 1 << i) for axis in reversed(GROUP) for i in range(int(math.log2(lax.axis_size(axis))))]
    for axis, k in rounds[:-1]:
        zpart = zpart + partner(zpart, axis, k)
    z, gram = gram_of(zpart, partner(zpart, *rounds[-1]))
    scale = math.sqrt(share * lax.axis_size(("col",) + GROUP))
    return solve(z, to_sum(gram, "col"), share, scale)


def solution(mesh):
    in_specs = (
        P(("dom", "row", "sub"), "col", None, None, None),
        P(("dom", "row", "sub"), "col", None),
        P(None, ("dom", "col", "row", "sub")),
    )
    out_specs = (P(None, ("dom", "col", "row", "sub")), P("dom", None))
    return jax.shard_map(body, mesh=mesh, in_specs=in_specs, out_specs=out_specs, check_vma=False)
```

```python
import math

import jax
import jax.numpy as jnp
from jax import lax
from jax.experimental import pallas as pl
from jax.experimental.pallas import tpu as pltpu
from jax.sharding import PartitionSpec as P

RBL = 4
LANES = 128
GROUP = ("row", "sub")
VMEM_LIMIT = 24 * 1024 * 1024

NT = (((1,), (1,)), ((), ()))
NN = (((1,), (0,)), ((), ()))


def params():
    return pltpu.CompilerParams(vmem_limit_bytes=VMEM_LIMIT)


def vmem():
    return pl.BlockSpec(memory_space=pltpu.VMEM)


def smem():
    return pl.BlockSpec(memory_space=pltpu.SMEM)


def halves(x):
    high = x.astype(jnp.bfloat16)
    low = (x - high.astype(jnp.float32)).astype(jnp.bfloat16)
    return high, low


def split_kernel(blocks_ref, high_ref, low_ref, held_ref, sems):
    count = blocks_ref.shape[0]
    copies = [pltpu.make_async_copy(blocks_ref.at[i], held_ref.at[i], sems.at[i]) for i in range(count)]
    for copy in copies:
        copy.start()
    for i, copy in enumerate(copies):
        copy.wait()
        high_ref[i], low_ref[i] = halves(held_ref[i])


def split_blocks(blocks):
    n, rows, cols = blocks.shape
    return pl.pallas_call(
        split_kernel,
        out_shape=(
            pltpu.VMEM(blocks.shape, jnp.bfloat16),
            pltpu.VMEM(blocks.shape, jnp.bfloat16),
        ),
        in_specs=[pl.BlockSpec(memory_space=pltpu.HBM)],
        out_specs=(vmem(), vmem()),
        scratch_shapes=[pltpu.VMEM(blocks.shape, jnp.float32), pltpu.SemaphoreType.DMA((n,))],
        compiler_params=params(),
        cost_estimate=pl.CostEstimate(flops=3 * n * rows * cols, bytes_accessed=8 * n * rows * cols, transcendentals=0),
    )(pltpu.with_memory_space_constraint(blocks, pltpu.HBM))


def store_halves(ref, index, x):
    count = x.shape[0]
    high, low = halves(x)
    ref[index, pl.ds(0, count)] = high
    ref[index, pl.ds(count, count)] = low


def product(pair, high, low, dims):
    count = pair.shape[0] // 2
    first = lax.dot_general(pair, high, dims, preferred_element_type=jnp.float32)
    second = lax.dot_general(pair[:count], low, dims, preferred_element_type=jnp.float32)
    return first[:count] + first[count:] + second


def rows_kernel(slot_ref, high_ref, low_ref, *refs):
    pieces, out_ref, pair_ref = refs[:-2], refs[-2], refs[-1]
    nblk, edge = high_ref.shape[0], high_ref.shape[1]
    per_piece = pieces[0].shape[1] // edge
    column_count = per_piece * len(pieces)
    me = lax.axis_index(GROUP)
    for k, piece in enumerate(pieces):
        for h in range(per_piece):
            store_halves(pair_ref, (me ^ k) * per_piece + h, piece[:, h * edge:(h + 1) * edge])
    out_ref[...] = jnp.zeros_like(out_ref)
    for b in range(nblk):
        slot = slot_ref[b]
        r, c = slot // column_count, slot % column_count
        out_ref[r] += product(pair_ref[c], high_ref[b], low_ref[b], NT)


def rows_product(slot, high, low, pieces):
    count = pieces[0].shape[0]
    nblk, edge = high.shape[0], high.shape[1]
    column_count = len(pieces) * pieces[0].shape[1] // edge
    return pl.pallas_call(
        rows_kernel,
        out_shape=jax.ShapeDtypeStruct((RBL, count, edge), jnp.float32),
        in_specs=[smem()] + [vmem()] * (2 + len(pieces)),
        out_specs=vmem(),
        scratch_shapes=[pltpu.VMEM((column_count, 2 * count, edge), jnp.bfloat16)],
        compiler_params=params(),
    )(slot, high, low, *pieces)


def cols_kernel(column_count, slot_ref, high_ref, low_ref, *refs):
    pieces, out_ref, pair_ref = refs[:-2], refs[-2], refs[-1]
    nblk = high_ref.shape[0]
    for r in range(RBL):
        total = pieces[0][r]
        for piece in pieces[1:]:
            total = total + piece[r]
        store_halves(pair_ref, r, total)
    out_ref[...] = jnp.zeros_like(out_ref)
    for b in range(nblk):
        slot = slot_ref[b]
        r, c = slot // column_count, slot % column_count
        out_ref[c] += product(pair_ref[r], high_ref[b], low_ref[b], NN)


def cols_product(slot, high, low, pieces, column_count):
    _, count, edge = pieces[0].shape
    return pl.pallas_call(
        lambda *refs: cols_kernel(column_count, *refs),
        out_shape=jax.ShapeDtypeStruct((column_count, count, edge), jnp.float32),
        in_specs=[smem()] + [vmem()] * (2 + len(pieces)),
        out_specs=vmem(),
        scratch_shapes=[pltpu.VMEM((RBL, 2 * count, edge), jnp.bfloat16)],
        compiler_params=params(),
    )(slot, high, low, *pieces)


def gram_kernel(a_ref, b_ref, z_ref, gram_ref):
    total = None
    for c in range(a_ref.shape[0]):
        z = a_ref[c] + b_ref[c]
        z_ref[c] = z
        g = lax.dot_general(z, z, NT, precision=lax.Precision.HIGHEST, preferred_element_type=jnp.float32)
        total = g if total is None else total + g
    gram_ref[...] = total


def gram_of(a, b):
    count = a.shape[1]
    return pl.pallas_call(
        gram_kernel,
        out_shape=(
            jax.ShapeDtypeStruct(a.shape, jnp.float32),
            jax.ShapeDtypeStruct((count, count), jnp.float32),
        ),
        in_specs=[vmem(), vmem()],
        out_specs=(vmem(), vmem()),
        compiler_params=params(),
    )(a, b)


def solve_kernel(scale, z_ref, *refs):
    grams, out_ref, factor_ref = refs[:-2], refs[-2], refs[-1]
    count, edge = factor_ref.shape[0], z_ref.shape[2]
    per_share = out_ref.shape[1] // edge
    first = lax.axis_index(GROUP) * per_share
    g = grams[0][...]
    for piece in grams[1:]:
        g = g + piece[...]
    z = [z_ref[first + h] for h in range(per_share)]
    row_id = lax.broadcasted_iota(jnp.int32, (count, LANES), 0)
    lane_id = lax.broadcasted_iota(jnp.int32, (count, LANES), 1)
    columns = [jnp.broadcast_to(g[:, k:k + 1], (count, LANES)) for k in range(count)]
    lower = jnp.zeros((count, LANES), jnp.float32)
    scales = jnp.zeros((count, LANES), jnp.float32)
    for j in range(count):
        column = columns[j]
        root = lax.rsqrt(column[j:j + 1, :])
        inverse = root * root
        lower = jnp.where((lane_id == j) & (row_id >= j), column * root, lower)
        scales = jnp.where(row_id == j, root, scales)
        below = jnp.where(row_id > j, column, 0.0)
        for k in range(j + 1, count):
            columns[k] = columns[k] - below * (column[k:k + 1, :] * inverse)
        if j + 1 < count:
            wide = jnp.concatenate([below] * (edge // LANES), 1)
            wide_inverse = jnp.concatenate([inverse] * (edge // LANES), 1)
            z = [x - wide * (x[j:j + 1, :] * wide_inverse) for x in z]
    scales = jnp.concatenate([scales * scale] * (edge // LANES), 1)
    for h in range(per_share):
        out_ref[:, h * edge:(h + 1) * edge] = z[h] * scales
    factor_ref[...] = lower[:, :count].T


def solve(z, grams, share, scale):
    count = z.shape[1]
    return pl.pallas_call(
        lambda *refs: solve_kernel(scale, *refs),
        out_shape=(
            jax.ShapeDtypeStruct((count, share), jnp.float32),
            jax.ShapeDtypeStruct((count, count), jnp.float32),
        ),
        in_specs=[vmem()] * (1 + len(grams)),
        out_specs=(vmem(), vmem()),
        compiler_params=params(),
    )(z, *grams)


def partner(x, axes, k):
    n = lax.axis_size(axes)
    return lax.ppermute(x, axes, [(i, i ^ k) for i in range(n)])


def is_power(n):
    return n & (n - 1) == 0


def gather(x, axes):
    n = lax.axis_size(axes)
    return [x] + [partner(x, axes, k) for k in range(1, n)]


def to_sum(x, axis):
    n = lax.axis_size(axis)
    if n <= 4 and is_power(n):
        return [x] + [partner(x, axis, k) for k in (3, 1, 2)]
    return [lax.psum(x, axis)]


def body(blocks, block_slot, basis_in):
    edge = blocks.shape[-1]
    nblk = blocks.shape[2]
    share = basis_in.shape[1]
    column_count = share * lax.axis_size(GROUP) // edge
    slot = block_slot.reshape(nblk)
    high, low = split_blocks(blocks.reshape(nblk, edge, edge))
    high = pltpu.with_memory_space_constraint(high, pltpu.VMEM)
    low = pltpu.with_memory_space_constraint(low, pltpu.VMEM)
    ypart = rows_product(slot, high, low, gather(basis_in, GROUP))
    zpart = cols_product(slot, high, low, to_sum(ypart, "col"), column_count)
    rounds = [(axis, 1 << i) for axis in reversed(GROUP) for i in range(int(math.log2(lax.axis_size(axis))))]
    for axis, k in rounds[:-1]:
        zpart = zpart + partner(zpart, axis, k)
    z, gram = gram_of(zpart, partner(zpart, *rounds[-1]))
    scale = math.sqrt(share * lax.axis_size(("col",) + GROUP))
    return solve(z, gather(gram, "col"), share, scale)


def solution(mesh):
    in_specs = (
        P(("dom", "row", "sub"), "col", None, None, None),
        P(("dom", "row", "sub"), "col", None),
        P(None, ("dom", "col", "row", "sub")),
    )
    out_specs = (P(None, ("dom", "col", "row", "sub")), P("dom", None))
    return jax.shard_map(body, mesh=mesh, in_specs=in_specs, out_specs=out_specs, check_vma=False)
```

```python
import math

import jax
import jax.numpy as jnp
from jax import lax
from jax.experimental import pallas as pl
from jax.experimental.pallas import tpu as pltpu
from jax.sharding import PartitionSpec as P

RBL = 4
LANES = 128
GROUP = ("row", "sub")
LEAD = 1
COLS = ((0, 1, 2, 3), (1, 0, 3, 2), (2, 3, 0, 1), (3, 2, 1, 0))
Y_ORDERS = ((3, 1, 2), (2, 3, 1))
G_ORDER = (3, 2, 1)
VMEM_LIMIT = 24 * 1024 * 1024

NT = (((1,), (1,)), ((), ()))
NN = (((1,), (0,)), ((), ()))


def params():
    return pltpu.CompilerParams(vmem_limit_bytes=VMEM_LIMIT)


def vmem():
    return pl.BlockSpec(memory_space=pltpu.VMEM)


def smem():
    return pl.BlockSpec(memory_space=pltpu.SMEM)


def halves(x):
    high = x.astype(jnp.bfloat16)
    low = (x - high.astype(jnp.float32)).astype(jnp.bfloat16)
    return high, low


def split_kernel(blocks_ref, high_ref, low_ref, high_t_ref, held_ref, sems):
    count = blocks_ref.shape[0]
    copies = [pltpu.make_async_copy(blocks_ref.at[i], held_ref.at[i], sems.at[i]) for i in range(count)]
    for copy in copies:
        copy.start()
    for i, copy in enumerate(copies):
        copy.wait()
        high, low = halves(held_ref[i])
        high_ref[i], low_ref[i] = high, low
        high_t_ref[i] = high.T


def split_blocks(blocks):
    n, rows, cols = blocks.shape
    return pl.pallas_call(
        split_kernel,
        out_shape=(
            pltpu.VMEM(blocks.shape, jnp.bfloat16),
            pltpu.VMEM(blocks.shape, jnp.bfloat16),
            pltpu.VMEM(blocks.shape, jnp.bfloat16),
        ),
        in_specs=[pl.BlockSpec(memory_space=pltpu.HBM)],
        out_specs=(vmem(), vmem(), vmem()),
        scratch_shapes=[pltpu.VMEM(blocks.shape, jnp.float32), pltpu.SemaphoreType.DMA((n,))],
        compiler_params=params(),
        cost_estimate=pl.CostEstimate(flops=3 * n * rows * cols, bytes_accessed=8 * n * rows * cols, transcendentals=0),
    )(pltpu.with_memory_space_constraint(blocks, pltpu.HBM))


def store_halves(ref, index, x):
    count = x.shape[0]
    high, low = halves(x)
    ref[index, pl.ds(0, count)] = high
    ref[index, pl.ds(count, count)] = low


def product(pair, high, low, dims, low_dims):
    count = pair.shape[0] // 2
    first = lax.dot_general(pair, high, dims, preferred_element_type=jnp.float32)
    second = lax.dot_general(pair[:count], low, low_dims, preferred_element_type=jnp.float32)
    return first[:count] + first[count:] + second


def rows_kernel(slot_ref, high_ref, low_ref, *refs):
    pieces, out_ref, pair_ref = refs[:-2], refs[-2], refs[-1]
    nblk, edge = high_ref.shape[0], high_ref.shape[1]
    per_piece = pieces[0].shape[1] // edge
    column_count = per_piece * len(pieces)
    me = lax.axis_index(GROUP)
    for k, piece in enumerate(pieces):
        for h in range(per_piece):
            store_halves(pair_ref, (me ^ k) * per_piece + h, piece[:, h * edge:(h + 1) * edge])
    out_ref[...] = jnp.zeros_like(out_ref)
    for b in range(nblk):
        slot = slot_ref[b]
        r, c = slot // column_count, slot % column_count
        out_ref[r] += product(pair_ref[c], high_ref[b], low_ref[b], NN, NT)


def rows_product(slot, high, low, pieces):
    count = pieces[0].shape[0]
    nblk, edge = high.shape[0], high.shape[1]
    column_count = len(pieces) * pieces[0].shape[1] // edge
    return pl.pallas_call(
        rows_kernel,
        out_shape=jax.ShapeDtypeStruct((RBL, count, edge), jnp.float32),
        in_specs=[smem()] + [vmem()] * (2 + len(pieces)),
        out_specs=vmem(),
        scratch_shapes=[pltpu.VMEM((column_count, 2 * count, edge), jnp.bfloat16)],
        compiler_params=params(),
    )(slot, high, low, *pieces)


def cols_kernel(column_count, slot_ref, high_ref, low_ref, *refs):
    pieces, out_ref, pair_ref = refs[:-2], refs[-2], refs[-1]
    nblk = high_ref.shape[0]
    for r in range(RBL):
        total = pieces[0][r]
        for piece in pieces[1:]:
            total = total + piece[r]
        store_halves(pair_ref, r, total)
    out_ref[...] = jnp.zeros_like(out_ref)
    for b in range(nblk):
        slot = slot_ref[b]
        r, c = slot // column_count, slot % column_count
        out_ref[c] += product(pair_ref[r], high_ref[b], low_ref[b], NN, NN)


def cols_product(slot, high, low, pieces, column_count):
    _, count, edge = pieces[0].shape
    return pl.pallas_call(
        lambda *refs: cols_kernel(column_count, *refs),
        out_shape=jax.ShapeDtypeStruct((column_count, count, edge), jnp.float32),
        in_specs=[smem()] + [vmem()] * (2 + len(pieces)),
        out_specs=vmem(),
        scratch_shapes=[pltpu.VMEM((RBL, 2 * count, edge), jnp.bfloat16)],
        compiler_params=params(),
    )(slot, high, low, *pieces)


def gram_kernel(lead, a_ref, b_ref, mine_ref, other_ref, gram_ref, z_ref):
    leads = True if lead is None else lax.axis_index("sub") == lead

    @pl.when(leads)
    def _():
        total = None
        for c in range(a_ref.shape[0]):
            z = a_ref[c] + b_ref[c]
            z_ref[c] = z
            g = lax.dot_general(z, z, NT, precision=lax.Precision.HIGHEST, preferred_element_type=jnp.float32)
            total = g if total is None else total + g
        gram_ref[...] = total
        me = lax.axis_index(GROUP)
        count = mine_ref.shape[0]
        for h in range(count):
            mine_ref[h] = z_ref[me * count + h]
            other_ref[h] = z_ref[(me ^ 1) * count + h]

    @pl.when(jnp.logical_not(leads))
    def _():
        gram_ref[...] = jnp.zeros_like(gram_ref)
        mine_ref[...] = jnp.zeros_like(mine_ref)
        other_ref[...] = jnp.zeros_like(other_ref)


def gram_of(a, b, per_share, lead):
    _, count, edge = a.shape
    share = jax.ShapeDtypeStruct((per_share, count, edge), jnp.float32)
    return pl.pallas_call(
        lambda *refs: gram_kernel(lead, *refs),
        out_shape=(share, share, jax.ShapeDtypeStruct((count, count), jnp.float32)),
        in_specs=[vmem(), vmem()],
        out_specs=(vmem(), vmem(), vmem()),
        scratch_shapes=[pltpu.VMEM(a.shape, jnp.float32)],
        compiler_params=params(),
    )(a, b)


def solve_kernel(scale, *refs):
    z_ref, gram_ref, out_ref, factor_ref = refs[0], refs[1], refs[-2], refs[-1]
    count, edge = factor_ref.shape[0], z_ref.shape[2]
    per_share = out_ref.shape[1] // edge
    g = gram_ref[...]
    z = [z_ref[h] for h in range(per_share)]
    if len(refs) > 4:
        leads = lax.axis_index("sub") == LEAD
        g = jnp.where(leads, g, refs[3][...])
        z = [jnp.where(leads, x, refs[2][h]) for h, x in enumerate(z)]
    row_id = lax.broadcasted_iota(jnp.int32, (count, LANES), 0)
    lane_id = lax.broadcasted_iota(jnp.int32, (count, LANES), 1)
    columns = [jnp.broadcast_to(g[:, k:k + 1], (count, LANES)) for k in range(count)]
    lower = jnp.zeros((count, LANES), jnp.float32)
    scales = jnp.zeros((count, LANES), jnp.float32)
    for j in range(count):
        column = columns[j]
        root = lax.rsqrt(column[j:j + 1, :])
        inverse = root * root
        lower = jnp.where((lane_id == j) & (row_id >= j), column * root, lower)
        scales = jnp.where(row_id == j, root, scales)
        below = jnp.where(row_id > j, column, 0.0)
        for k in range(j + 1, count):
            columns[k] = columns[k] - below * (column[k:k + 1, :] * inverse)
        if j + 1 < count:
            wide = jnp.concatenate([below] * (edge // LANES), 1)
            wide_inverse = jnp.concatenate([inverse] * (edge // LANES), 1)
            z = [x - wide * (x[j:j + 1, :] * wide_inverse) for x in z]
    scales = jnp.concatenate([scales * scale] * (edge // LANES), 1)
    for h in range(per_share):
        out_ref[:, h * edge:(h + 1) * edge] = z[h] * scales
    factor_ref[...] = lower[:, :count].T


def solve(scale, *arrays):
    per_share, count, edge = arrays[0].shape
    return pl.pallas_call(
        lambda *refs: solve_kernel(scale, *refs),
        out_shape=(
            jax.ShapeDtypeStruct((count, per_share * edge), jnp.float32),
            jax.ShapeDtypeStruct((count, count), jnp.float32),
        ),
        in_specs=[vmem()] * len(arrays),
        out_specs=(vmem(), vmem()),
        compiler_params=params(),
    )(*arrays)


def partner(x, axes, k):
    n = lax.axis_size(axes)
    return lax.ppermute(x, axes, [(i, i ^ k) for i in range(n)])


def is_power(n):
    return n & (n - 1) == 0


def gather(x, axes):
    n = lax.axis_size(axes)
    return [x] + [partner(x, axes, k) for k in range(1, n)]


def exchange(x, steps):
    cols, rows, subs = (lax.axis_size(a) for a in ("col", "row", "sub"))
    place = lambda c, r, s: (c * rows + r) * subs + s
    pairs = [
        (place(c, r, s), place(steps[s][0][c], r ^ steps[s][1], s))
        for c in range(cols)
        for r in range(rows)
        for s in range(subs)
    ]
    return lax.ppermute(x, ("col", "row", "sub"), pairs)


def general(slot, high, low, ypart, column_count, per_share, scale):
    zpart = cols_product(slot, high, low, [lax.psum(ypart, "col")], column_count)
    for axis in ("sub", "row"):
        n = lax.axis_size(axis)
        if is_power(n):
            for i in range(n.bit_length() - 1):
                zpart = zpart + partner(zpart, axis, 1 << i)
        else:
            zpart = lax.psum(zpart, axis)
    z, _, gram = gram_of(zpart, jnp.zeros_like(zpart), per_share, None)
    return solve(scale, z, lax.psum(gram, "col"))


def four_by_two(slot, high, low, ypart, column_count, per_share, scale):
    ypieces = [ypart] + [exchange(ypart, ((COLS[a], 0), (COLS[b], 0))) for a, b in zip(*Y_ORDERS)]
    zpart = cols_product(slot, high, low, ypieces, column_count)
    zpart = zpart + partner(zpart, "sub", 1)
    z, other, gram = gram_of(zpart, exchange(zpart, ((COLS[1], 0), (COLS[0], 1))), per_share, LEAD)
    far_z = partner(other, "sub", 1)
    gram = gram + sum(exchange(gram, ((COLS[0], 1), (COLS[k], 0))) for k in G_ORDER)
    return solve(scale, z, gram, far_z, partner(gram, "sub", 1))


def body(blocks, block_slot, basis_in):
    edge = blocks.shape[-1]
    nblk = blocks.shape[2]
    share = basis_in.shape[1]
    column_count = share * lax.axis_size(GROUP) // edge
    slot = block_slot.reshape(nblk)
    high, low, high_t = [
        pltpu.with_memory_space_constraint(x, pltpu.VMEM) for x in split_blocks(blocks.reshape(nblk, edge, edge))
    ]
    ypart = rows_product(slot, high_t, low, gather(basis_in, GROUP))
    scale = math.sqrt(share * lax.axis_size(("col",) + GROUP))
    sizes = tuple(lax.axis_size(a) for a in ("col", "row", "sub"))
    finish = four_by_two if sizes == (4, 2, 2) else general
    return finish(slot, high, low, ypart, column_count, share // edge, scale)


def solution(mesh):
    in_specs = (
        P(("dom", "row", "sub"), "col", None, None, None),
        P(("dom", "row", "sub"), "col", None),
        P(None, ("dom", "col", "row", "sub")),
    )
    out_specs = (P(None, ("dom", "col", "row", "sub")), P("dom", None))
    return jax.shard_map(body, mesh=mesh, in_specs=in_specs, out_specs=out_specs, check_vma=False)
```

```python
import math

import jax
import jax.numpy as jnp
from jax import lax
from jax.experimental import pallas as pl
from jax.experimental.pallas import tpu as pltpu
from jax.sharding import PartitionSpec as P

RBL = 4
LANES = 128
GROUP = ("row", "sub")
LEAD = 1
COLS = ((0, 1, 2, 3), (1, 0, 3, 2), (2, 3, 0, 1), (3, 2, 1, 0))
Y_ORDERS = ((3, 1, 2), (2, 3, 1))
G_ORDER = (3, 2, 1)
VMEM_LIMIT = 24 * 1024 * 1024

NT = (((1,), (1,)), ((), ()))
NN = (((1,), (0,)), ((), ()))


def params():
    return pltpu.CompilerParams(vmem_limit_bytes=VMEM_LIMIT)


def vmem():
    return pl.BlockSpec(memory_space=pltpu.VMEM)


def smem():
    return pl.BlockSpec(memory_space=pltpu.SMEM)


def halves(x):
    high = x.astype(jnp.bfloat16)
    low = (x - high.astype(jnp.float32)).astype(jnp.bfloat16)
    return high, low


def split_kernel(blocks_ref, slot_ref, high_ref, low_ref, high_t_ref, place_ref, held_ref, sems, slot_sem):
    count = blocks_ref.shape[0]
    place = pltpu.make_async_copy(slot_ref, place_ref, slot_sem)
    place.start()
    copies = [pltpu.make_async_copy(blocks_ref.at[i], held_ref.at[i], sems.at[i]) for i in range(count)]
    for copy in copies:
        copy.start()
    for i, copy in enumerate(copies):
        copy.wait()
        high, low = halves(held_ref[i])
        high_ref[i], low_ref[i] = high, low
        high_t_ref[i] = high.T
    place.wait()


def split_blocks(blocks, slot):
    n, rows, cols = blocks.shape
    return pl.pallas_call(
        split_kernel,
        out_shape=(
            pltpu.VMEM(blocks.shape, jnp.bfloat16),
            pltpu.VMEM(blocks.shape, jnp.bfloat16),
            pltpu.VMEM(blocks.shape, jnp.bfloat16),
            pltpu.SMEM(slot.shape, jnp.int32),
        ),
        in_specs=[pl.BlockSpec(memory_space=pltpu.HBM)] * 2,
        out_specs=(vmem(), vmem(), vmem(), smem()),
        scratch_shapes=[
            pltpu.VMEM(blocks.shape, jnp.float32),
            pltpu.SemaphoreType.DMA((n,)),
            pltpu.SemaphoreType.DMA,
        ],
        compiler_params=params(),
        cost_estimate=pl.CostEstimate(flops=3 * n * rows * cols, bytes_accessed=8 * n * rows * cols, transcendentals=0),
    )(*[pltpu.with_memory_space_constraint(x, pltpu.HBM) for x in (blocks, slot)])


def store_halves(ref, index, x):
    count = x.shape[0]
    high, low = halves(x)
    ref[index, pl.ds(0, count)] = high
    ref[index, pl.ds(count, count)] = low


def product(pair, high, low, dims, low_dims):
    count = pair.shape[0] // 2
    first = lax.dot_general(pair, high, dims, preferred_element_type=jnp.float32)
    second = lax.dot_general(pair[:count], low, low_dims, preferred_element_type=jnp.float32)
    return first[:count] + first[count:] + second


def rows_kernel(slot_ref, high_ref, low_ref, *refs):
    pieces, out_ref, pair_ref = refs[:-2], refs[-2], refs[-1]
    nblk, edge = high_ref.shape[0], high_ref.shape[1]
    per_piece = pieces[0].shape[1] // edge
    column_count = per_piece * len(pieces)
    me = lax.axis_index(GROUP)
    for k, piece in enumerate(pieces):
        for h in range(per_piece):
            store_halves(pair_ref, (me ^ k) * per_piece + h, piece[:, h * edge:(h + 1) * edge])
    out_ref[...] = jnp.zeros_like(out_ref)
    for b in range(nblk):
        slot = slot_ref[b]
        r, c = slot // column_count, slot % column_count
        out_ref[r] += product(pair_ref[c], high_ref[b], low_ref[b], NN, NT)


def rows_product(slot, high, low, pieces):
    count = pieces[0].shape[0]
    nblk, edge = high.shape[0], high.shape[1]
    column_count = len(pieces) * pieces[0].shape[1] // edge
    return pl.pallas_call(
        rows_kernel,
        out_shape=jax.ShapeDtypeStruct((RBL, count, edge), jnp.float32),
        in_specs=[smem()] + [vmem()] * (2 + len(pieces)),
        out_specs=vmem(),
        scratch_shapes=[pltpu.VMEM((column_count, 2 * count, edge), jnp.bfloat16)],
        compiler_params=params(),
    )(slot, high, low, *pieces)


def cols_kernel(column_count, slot_ref, high_ref, low_ref, *refs):
    pieces, out_ref, pair_ref = refs[:-2], refs[-2], refs[-1]
    nblk = high_ref.shape[0]
    for r in range(RBL):
        total = pieces[0][r]
        for piece in pieces[1:]:
            total = total + piece[r]
        store_halves(pair_ref, r, total)
    out_ref[...] = jnp.zeros_like(out_ref)
    for b in range(nblk):
        slot = slot_ref[b]
        r, c = slot // column_count, slot % column_count
        out_ref[c] += product(pair_ref[r], high_ref[b], low_ref[b], NN, NN)


def cols_product(slot, high, low, pieces, column_count):
    _, count, edge = pieces[0].shape
    return pl.pallas_call(
        lambda *refs: cols_kernel(column_count, *refs),
        out_shape=jax.ShapeDtypeStruct((column_count, count, edge), jnp.float32),
        in_specs=[smem()] + [vmem()] * (2 + len(pieces)),
        out_specs=vmem(),
        scratch_shapes=[pltpu.VMEM((RBL, 2 * count, edge), jnp.bfloat16)],
        compiler_params=params(),
    )(slot, high, low, *pieces)


def gram_kernel(lead, a_ref, b_ref, mine_ref, other_ref, gram_ref, z_ref):
    leads = True if lead is None else lax.axis_index("sub") == lead

    @pl.when(leads)
    def _():
        total = None
        for c in range(a_ref.shape[0]):
            z = a_ref[c] + b_ref[c]
            z_ref[c] = z
            g = lax.dot_general(z, z, NT, precision=lax.Precision.HIGHEST, preferred_element_type=jnp.float32)
            total = g if total is None else total + g
        gram_ref[...] = total
        me = lax.axis_index(GROUP)
        count = mine_ref.shape[0]
        for h in range(count):
            mine_ref[h] = z_ref[me * count + h]
            other_ref[h] = z_ref[(me ^ 1) * count + h]

    @pl.when(jnp.logical_not(leads))
    def _():
        gram_ref[...] = jnp.zeros_like(gram_ref)
        mine_ref[...] = jnp.zeros_like(mine_ref)
        other_ref[...] = jnp.zeros_like(other_ref)


def gram_of(a, b, per_share, lead):
    _, count, edge = a.shape
    share = jax.ShapeDtypeStruct((per_share, count, edge), jnp.float32)
    return pl.pallas_call(
        lambda *refs: gram_kernel(lead, *refs),
        out_shape=(share, share, jax.ShapeDtypeStruct((count, count), jnp.float32)),
        in_specs=[vmem(), vmem()],
        out_specs=(vmem(), vmem(), vmem()),
        scratch_shapes=[pltpu.VMEM(a.shape, jnp.float32)],
        compiler_params=params(),
    )(a, b)


def solve_kernel(scale, *refs):
    z_ref, gram_ref, out_ref, factor_ref = refs[0], refs[1], refs[-2], refs[-1]
    count, edge = factor_ref.shape[0], z_ref.shape[2]
    per_share = out_ref.shape[1] // edge
    g = gram_ref[...]
    z = [z_ref[h] for h in range(per_share)]
    if len(refs) > 4:
        leads = lax.axis_index("sub") == LEAD
        g = jnp.where(leads, g, refs[3][...])
        z = [jnp.where(leads, x, refs[2][h]) for h, x in enumerate(z)]
    row_id = lax.broadcasted_iota(jnp.int32, (count, LANES), 0)
    lane_id = lax.broadcasted_iota(jnp.int32, (count, LANES), 1)
    columns = [jnp.broadcast_to(g[:, k:k + 1], (count, LANES)) for k in range(count)]
    lower = jnp.zeros((count, LANES), jnp.float32)
    scales = jnp.zeros((count, LANES), jnp.float32)
    for j in range(count):
        column = columns[j]
        root = lax.rsqrt(column[j:j + 1, :])
        inverse = root * root
        lower = jnp.where((lane_id == j) & (row_id >= j), column * root, lower)
        scales = jnp.where(row_id == j, root, scales)
        below = jnp.where(row_id > j, column, 0.0)
        for k in range(j + 1, count):
            columns[k] = columns[k] - below * (column[k:k + 1, :] * inverse)
        if j + 1 < count:
            wide = jnp.concatenate([below] * (edge // LANES), 1)
            wide_inverse = jnp.concatenate([inverse] * (edge // LANES), 1)
            z = [x - wide * (x[j:j + 1, :] * wide_inverse) for x in z]
    scales = jnp.concatenate([scales * scale] * (edge // LANES), 1)
    for h in range(per_share):
        out_ref[:, h * edge:(h + 1) * edge] = z[h] * scales
    factor_ref[...] = lower[:, :count].T


def solve(scale, *arrays):
    per_share, count, edge = arrays[0].shape
    return pl.pallas_call(
        lambda *refs: solve_kernel(scale, *refs),
        out_shape=(
            jax.ShapeDtypeStruct((count, per_share * edge), jnp.float32),
            jax.ShapeDtypeStruct((count, count), jnp.float32),
        ),
        in_specs=[vmem()] * len(arrays),
        out_specs=(vmem(), vmem()),
        compiler_params=params(),
    )(*arrays)


def partner(x, axes, k):
    n = lax.axis_size(axes)
    return lax.ppermute(x, axes, [(i, i ^ k) for i in range(n)])


def is_power(n):
    return n & (n - 1) == 0


def gather(x, axes):
    n = lax.axis_size(axes)
    return [x] + [partner(x, axes, k) for k in range(1, n)]


def exchange(x, steps):
    cols, rows, subs = (lax.axis_size(a) for a in ("col", "row", "sub"))
    place = lambda c, r, s: (c * rows + r) * subs + s
    pairs = [
        (place(c, r, s), place(steps[s][0][c], r ^ steps[s][1], s))
        for c in range(cols)
        for r in range(rows)
        for s in range(subs)
    ]
    return lax.ppermute(x, ("col", "row", "sub"), pairs)


def general(slot, high, low, ypart, column_count, per_share, scale):
    zpart = cols_product(slot, high, low, [lax.psum(ypart, "col")], column_count)
    for axis in ("sub", "row"):
        n = lax.axis_size(axis)
        if is_power(n):
            for i in range(n.bit_length() - 1):
                zpart = zpart + partner(zpart, axis, 1 << i)
        else:
            zpart = lax.psum(zpart, axis)
    z, _, gram = gram_of(zpart, jnp.zeros_like(zpart), per_share, None)
    return solve(scale, z, lax.psum(gram, "col"))


def four_by_two(slot, high, low, ypart, column_count, per_share, scale):
    ypieces = [ypart] + [exchange(ypart, ((COLS[a], 0), (COLS[b], 0))) for a, b in zip(*Y_ORDERS)]
    zpart = cols_product(slot, high, low, ypieces, column_count)
    zpart = zpart + partner(zpart, "sub", 1)
    z, other, gram = gram_of(zpart, exchange(zpart, ((COLS[1], 0), (COLS[0], 1))), per_share, LEAD)
    far_z = partner(other, "sub", 1)
    gram = gram + sum(exchange(gram, ((COLS[0], 1), (COLS[k], 0))) for k in G_ORDER)
    return solve(scale, z, gram, far_z, partner(gram, "sub", 1))


def body(blocks, block_slot, basis_in):
    edge = blocks.shape[-1]
    nblk = blocks.shape[2]
    share = basis_in.shape[1]
    column_count = share * lax.axis_size(GROUP) // edge
    slot = block_slot.reshape(nblk)
    *split, slot = split_blocks(blocks.reshape(nblk, edge, edge), slot)
    high, low, high_t = [pltpu.with_memory_space_constraint(x, pltpu.VMEM) for x in split]
    slot = pltpu.with_memory_space_constraint(slot, pltpu.SMEM)
    ypart = rows_product(slot, high_t, low, gather(basis_in, GROUP))
    scale = math.sqrt(share * lax.axis_size(("col",) + GROUP))
    sizes = tuple(lax.axis_size(a) for a in ("col", "row", "sub"))
    finish = four_by_two if sizes == (4, 2, 2) else general
    return finish(slot, high, low, ypart, column_count, share // edge, scale)


def solution(mesh):
    in_specs = (
        P(("dom", "row", "sub"), "col", None, None, None),
        P(("dom", "row", "sub"), "col", None),
        P(None, ("dom", "col", "row", "sub")),
    )
    out_specs = (P(None, ("dom", "col", "row", "sub")), P("dom", None))
    return jax.shard_map(body, mesh=mesh, in_specs=in_specs, out_specs=out_specs, check_vma=False)
```

```python
import math

import jax
import jax.numpy as jnp
from jax import lax
from jax.experimental import pallas as pl
from jax.experimental.pallas import tpu as pltpu
from jax.sharding import PartitionSpec as P

RBL = 4
LANES = 128
GROUP = ("row", "sub")
LEAD = 1
COLS = ((0, 1, 2, 3), (1, 0, 3, 2), (2, 3, 0, 1), (3, 2, 1, 0), (1, 3, 0, 2), (2, 0, 3, 1))
Y_ORDERS = ((3, 1, 2), (2, 3, 1))
G_ORDER = (4, 3, 5)
VMEM_LIMIT = 24 * 1024 * 1024

NT = (((1,), (1,)), ((), ()))
NN = (((1,), (0,)), ((), ()))


def params():
    return pltpu.CompilerParams(vmem_limit_bytes=VMEM_LIMIT)


def vmem():
    return pl.BlockSpec(memory_space=pltpu.VMEM)


def smem():
    return pl.BlockSpec(memory_space=pltpu.SMEM)


def halves(x):
    high = x.astype(jnp.bfloat16)
    low = (x - high.astype(jnp.float32)).astype(jnp.bfloat16)
    return high, low


def split_kernel(blocks_ref, slot_ref, high_ref, low_ref, high_t_ref, place_ref, held_ref, sems, slot_sem):
    count = blocks_ref.shape[0]
    place = pltpu.make_async_copy(slot_ref, place_ref, slot_sem)
    place.start()
    copies = [pltpu.make_async_copy(blocks_ref.at[i], held_ref.at[i], sems.at[i]) for i in range(count)]
    for copy in copies:
        copy.start()
    for i, copy in enumerate(copies):
        copy.wait()
        high, low = halves(held_ref[i])
        high_ref[i], low_ref[i] = high, low
        high_t_ref[i] = high.T
    place.wait()


def split_blocks(blocks, slot):
    n, rows, cols = blocks.shape
    return pl.pallas_call(
        split_kernel,
        out_shape=(
            pltpu.VMEM(blocks.shape, jnp.bfloat16),
            pltpu.VMEM(blocks.shape, jnp.bfloat16),
            pltpu.VMEM(blocks.shape, jnp.bfloat16),
            pltpu.SMEM(slot.shape, jnp.int32),
        ),
        in_specs=[pl.BlockSpec(memory_space=pltpu.HBM)] * 2,
        out_specs=(vmem(), vmem(), vmem(), smem()),
        scratch_shapes=[
            pltpu.VMEM(blocks.shape, jnp.float32),
            pltpu.SemaphoreType.DMA((n,)),
            pltpu.SemaphoreType.DMA,
        ],
        compiler_params=params(),
        cost_estimate=pl.CostEstimate(flops=3 * n * rows * cols, bytes_accessed=8 * n * rows * cols, transcendentals=0),
    )(*[pltpu.with_memory_space_constraint(x, pltpu.HBM) for x in (blocks, slot)])


def store_halves(ref, index, x):
    count = x.shape[0]
    high, low = halves(x)
    ref[index, pl.ds(0, count)] = high
    ref[index, pl.ds(count, count)] = low


def product(pair, high, low, dims, low_dims):
    count = pair.shape[0] // 2
    first = lax.dot_general(pair, high, dims, preferred_element_type=jnp.float32)
    second = lax.dot_general(pair[:count], low, low_dims, preferred_element_type=jnp.float32)
    return first[:count] + first[count:] + second


def rows_kernel(slot_ref, high_ref, low_ref, *refs):
    pieces, out_ref, pair_ref = refs[:-2], refs[-2], refs[-1]
    nblk, edge = high_ref.shape[0], high_ref.shape[1]
    per_piece = pieces[0].shape[1] // edge
    column_count = per_piece * len(pieces)
    me = lax.axis_index(GROUP)
    for k, piece in enumerate(pieces):
        for h in range(per_piece):
            store_halves(pair_ref, (me ^ k) * per_piece + h, piece[:, h * edge:(h + 1) * edge])
    out_ref[...] = jnp.zeros_like(out_ref)
    for b in range(nblk):
        slot = slot_ref[b]
        r, c = slot // column_count, slot % column_count
        out_ref[r] += product(pair_ref[c], high_ref[b], low_ref[b], NN, NT)


def rows_product(slot, high, low, pieces):
    count = pieces[0].shape[0]
    nblk, edge = high.shape[0], high.shape[1]
    column_count = len(pieces) * pieces[0].shape[1] // edge
    return pl.pallas_call(
        rows_kernel,
        out_shape=jax.ShapeDtypeStruct((RBL, count, edge), jnp.float32),
        in_specs=[smem()] + [vmem()] * (2 + len(pieces)),
        out_specs=vmem(),
        scratch_shapes=[pltpu.VMEM((column_count, 2 * count, edge), jnp.bfloat16)],
        compiler_params=params(),
    )(slot, high, low, *pieces)


def cols_kernel(column_count, slot_ref, high_ref, low_ref, *refs):
    pieces, out_ref, pair_ref = refs[:-2], refs[-2], refs[-1]
    nblk = high_ref.shape[0]
    for r in range(RBL):
        total = pieces[0][r]
        for piece in pieces[1:]:
            total = total + piece[r]
        store_halves(pair_ref, r, total)
    out_ref[...] = jnp.zeros_like(out_ref)
    for b in range(nblk):
        slot = slot_ref[b]
        r, c = slot // column_count, slot % column_count
        out_ref[c] += product(pair_ref[r], high_ref[b], low_ref[b], NN, NN)


def cols_product(slot, high, low, pieces, column_count):
    _, count, edge = pieces[0].shape
    return pl.pallas_call(
        lambda *refs: cols_kernel(column_count, *refs),
        out_shape=jax.ShapeDtypeStruct((column_count, count, edge), jnp.float32),
        in_specs=[smem()] + [vmem()] * (2 + len(pieces)),
        out_specs=vmem(),
        scratch_shapes=[pltpu.VMEM((RBL, 2 * count, edge), jnp.bfloat16)],
        compiler_params=params(),
    )(slot, high, low, *pieces)


def gram_kernel(lead, a_ref, b_ref, mine_ref, other_ref, gram_ref, z_ref):
    leads = True if lead is None else lax.axis_index("sub") == lead

    @pl.when(leads)
    def _():
        total = None
        for c in range(a_ref.shape[0]):
            z = a_ref[c] + b_ref[c]
            z_ref[c] = z
            g = lax.dot_general(z, z, NT, precision=lax.Precision.HIGHEST, preferred_element_type=jnp.float32)
            total = g if total is None else total + g
        gram_ref[...] = total
        me = lax.axis_index(GROUP)
        count = mine_ref.shape[0]
        for h in range(count):
            mine_ref[h] = z_ref[me * count + h]
            other_ref[h] = z_ref[(me ^ 1) * count + h]

    @pl.when(jnp.logical_not(leads))
    def _():
        gram_ref[...] = jnp.zeros_like(gram_ref)
        mine_ref[...] = jnp.zeros_like(mine_ref)
        other_ref[...] = jnp.zeros_like(other_ref)


def gram_of(a, b, per_share, lead):
    _, count, edge = a.shape
    share = jax.ShapeDtypeStruct((per_share, count, edge), jnp.float32)
    return pl.pallas_call(
        lambda *refs: gram_kernel(lead, *refs),
        out_shape=(share, share, jax.ShapeDtypeStruct((count, count), jnp.float32)),
        in_specs=[vmem(), vmem()],
        out_specs=(vmem(), vmem(), vmem()),
        scratch_shapes=[pltpu.VMEM(a.shape, jnp.float32)],
        compiler_params=params(),
    )(a, b)


def eliminate(g, z, scale):
    count, edge = g.shape[0], z[0].shape[1]
    row_id = lax.broadcasted_iota(jnp.int32, (count, LANES), 0)
    lane_id = lax.broadcasted_iota(jnp.int32, (count, LANES), 1)
    columns = [jnp.broadcast_to(g[:, k:k + 1], (count, LANES)) for k in range(count)]
    lower = jnp.zeros((count, LANES), jnp.float32)
    scales = jnp.zeros((count, LANES), jnp.float32)
    for j in range(count):
        column = columns[j]
        root = lax.rsqrt(column[j:j + 1, :])
        inverse = root * root
        lower = jnp.where((lane_id == j) & (row_id >= j), column * root, lower)
        scales = jnp.where(row_id == j, root, scales)
        below = jnp.where(row_id > j, column, 0.0)
        for k in range(j + 1, count):
            columns[k] = columns[k] - below * (column[k:k + 1, :] * inverse)
        if j + 1 < count:
            wide = jnp.concatenate([below] * (edge // LANES), 1)
            wide_inverse = jnp.concatenate([inverse] * (edge // LANES), 1)
            z = [x - wide * (x[j:j + 1, :] * wide_inverse) for x in z]
    scales = jnp.concatenate([scales * scale] * (edge // LANES), 1)
    return lower[:, :count].T, [x * scales for x in z]


def solve_kernel(scale, lead, z_ref, far_z_ref, *refs):
    grams, mine_ref, other_ref = refs[:-2], refs[-2], refs[-1]
    leads = True if lead is None else lax.axis_index("sub") == lead
    per_share, count, edge = z_ref.shape

    @pl.when(leads)
    def _():
        g = grams[0][...]
        for ref in grams[1:]:
            g = g + ref[...]
        factor, z = eliminate(g, [ref[h] for ref in (z_ref, far_z_ref) for h in range(per_share)], scale)
        for h in range(per_share):
            mine_ref[:, h * edge:(h + 1) * edge] = z[h]
            other_ref[:, h * edge:(h + 1) * edge] = z[per_share + h]
        other_ref[:, per_share * edge:] = jnp.zeros((count, LANES), jnp.float32)
        other_ref[:, per_share * edge:per_share * edge + count] = factor

    @pl.when(jnp.logical_not(leads))
    def _():
        mine_ref[...] = jnp.zeros_like(mine_ref)
        other_ref[...] = jnp.zeros_like(other_ref)


def solve(scale, lead, z, far_z, grams):
    per_share, count, edge = z.shape
    share = per_share * edge
    return pl.pallas_call(
        lambda *refs: solve_kernel(scale, lead, *refs),
        out_shape=(
            jax.ShapeDtypeStruct((count, share), jnp.float32),
            jax.ShapeDtypeStruct((count, share + LANES), jnp.float32),
        ),
        in_specs=[vmem()] * (2 + len(grams)),
        out_specs=(vmem(), vmem()),
        compiler_params=params(),
    )(z, far_z, *grams)


def pick_kernel(mine_ref, other_ref, far_ref, out_ref, factor_ref):
    leads = lax.axis_index("sub") == LEAD
    share, count = out_ref.shape[1], factor_ref.shape[0]
    out_ref[...] = jnp.where(leads, mine_ref[...], far_ref[:, :share])
    factor_ref[...] = jnp.where(leads, other_ref[:, share:share + count], far_ref[:, share:share + count])


def pick(mine, other, far):
    count, share = mine.shape
    return pl.pallas_call(
        pick_kernel,
        out_shape=(
            jax.ShapeDtypeStruct((count, share), jnp.float32),
            jax.ShapeDtypeStruct((count, count), jnp.float32),
        ),
        in_specs=[vmem()] * 3,
        out_specs=(vmem(), vmem()),
        compiler_params=params(),
    )(mine, other, far)


def partner(x, axes, k):
    n = lax.axis_size(axes)
    return lax.ppermute(x, axes, [(i, i ^ k) for i in range(n)])


def is_power(n):
    return n & (n - 1) == 0


def gather(x, axes):
    n = lax.axis_size(axes)
    return [x] + [partner(x, axes, k) for k in range(1, n)]


def exchange(x, steps):
    cols, rows, subs = (lax.axis_size(a) for a in ("col", "row", "sub"))
    place = lambda c, r, s: (c * rows + r) * subs + s
    pairs = [
        (place(c, r, s), place(steps[s][0][c], r ^ steps[s][1], s))
        for c in range(cols)
        for r in range(rows)
        for s in range(subs)
    ]
    return lax.ppermute(x, ("col", "row", "sub"), pairs)


def general(slot, high, low, ypart, column_count, per_share, scale):
    zpart = cols_product(slot, high, low, [lax.psum(ypart, "col")], column_count)
    for axis in ("sub", "row"):
        n = lax.axis_size(axis)
        if is_power(n):
            for i in range(n.bit_length() - 1):
                zpart = zpart + partner(zpart, axis, 1 << i)
        else:
            zpart = lax.psum(zpart, axis)
    z, other, gram = gram_of(zpart, jnp.zeros_like(zpart), per_share, None)
    mine, other = solve(scale, None, z, other, [lax.psum(gram, "col")])
    return mine, other[:, mine.shape[1]:mine.shape[1] + gram.shape[0]]


def four_by_two(slot, high, low, ypart, column_count, per_share, scale):
    ypieces = [ypart] + [exchange(ypart, ((COLS[a], 0), (COLS[b], 0))) for a, b in zip(*Y_ORDERS)]
    zpart = cols_product(slot, high, low, ypieces, column_count)
    zpart = zpart + partner(zpart, "sub", 1)
    z, other, gram = gram_of(zpart, exchange(zpart, ((COLS[1], 0), (COLS[0], 1))), per_share, LEAD)
    grams = [gram] + [exchange(gram, ((COLS[0], 1), (COLS[k], 0))) for k in G_ORDER]
    mine, other = solve(scale, LEAD, z, other, grams)
    return pick(mine, other, partner(other, "sub", 1))


def body(blocks, block_slot, basis_in):
    edge = blocks.shape[-1]
    nblk = blocks.shape[2]
    share = basis_in.shape[1]
    column_count = share * lax.axis_size(GROUP) // edge
    slot = block_slot.reshape(nblk)
    *split, slot = split_blocks(blocks.reshape(nblk, edge, edge), slot)
    high, low, high_t = [pltpu.with_memory_space_constraint(x, pltpu.VMEM) for x in split]
    slot = pltpu.with_memory_space_constraint(slot, pltpu.SMEM)
    ypart = rows_product(slot, high_t, low, gather(basis_in, GROUP))
    scale = math.sqrt(share * lax.axis_size(("col",) + GROUP))
    sizes = tuple(lax.axis_size(a) for a in ("col", "row", "sub"))
    finish = four_by_two if sizes == (4, 2, 2) else general
    return finish(slot, high, low, ypart, column_count, share // edge, scale)


def solution(mesh):
    in_specs = (
        P(("dom", "row", "sub"), "col", None, None, None),
        P(("dom", "row", "sub"), "col", None),
        P(None, ("dom", "col", "row", "sub")),
    )
    out_specs = (P(None, ("dom", "col", "row", "sub")), P("dom", None))
    return jax.shard_map(body, mesh=mesh, in_specs=in_specs, out_specs=out_specs, check_vma=False)
```

```python
import math

import jax
import jax.numpy as jnp
from jax import lax
from jax.experimental import pallas as pl
from jax.experimental.pallas import tpu as pltpu
from jax.sharding import PartitionSpec as P

RBL = 4
LANES = 128
GROUP = ("row", "sub")
LEAD = 1
COLS = ((0, 1, 2, 3), (1, 0, 3, 2), (2, 3, 0, 1), (3, 2, 1, 0), (1, 3, 0, 2), (2, 0, 3, 1))
Y_ORDERS = ((3, 1, 2), (2, 3, 1))
G_ORDER = (4, 3, 5)
VMEM_LIMIT = 24 * 1024 * 1024

NT = (((1,), (1,)), ((), ()))
NN = (((1,), (0,)), ((), ()))


def params():
    return pltpu.CompilerParams(vmem_limit_bytes=VMEM_LIMIT)


def vmem():
    return pl.BlockSpec(memory_space=pltpu.VMEM)


def smem():
    return pl.BlockSpec(memory_space=pltpu.SMEM)


def halves(x):
    high = x.astype(jnp.bfloat16)
    low = (x - high.astype(jnp.float32)).astype(jnp.bfloat16)
    return high, low


def split_kernel(blocks_ref, slot_ref, high_ref, low_ref, high_t_ref, place_ref, held_ref, sems, slot_sem):
    count = blocks_ref.shape[0]
    place = pltpu.make_async_copy(slot_ref, place_ref, slot_sem)
    place.start()
    copies = [pltpu.make_async_copy(blocks_ref.at[i], held_ref.at[i], sems.at[i]) for i in range(count)]
    for copy in copies:
        copy.start()
    for i, copy in enumerate(copies):
        copy.wait()
        high, low = halves(held_ref[i])
        high_ref[i], low_ref[i] = high, low
        high_t_ref[i] = high.T
    place.wait()


def split_blocks(blocks, slot):
    n, rows, cols = blocks.shape
    return pl.pallas_call(
        split_kernel,
        out_shape=(
            pltpu.VMEM(blocks.shape, jnp.bfloat16),
            pltpu.VMEM(blocks.shape, jnp.bfloat16),
            pltpu.VMEM(blocks.shape, jnp.bfloat16),
            pltpu.SMEM(slot.shape, jnp.int32),
        ),
        in_specs=[pl.BlockSpec(memory_space=pltpu.HBM)] * 2,
        out_specs=(vmem(), vmem(), vmem(), smem()),
        scratch_shapes=[
            pltpu.VMEM(blocks.shape, jnp.float32),
            pltpu.SemaphoreType.DMA((n,)),
            pltpu.SemaphoreType.DMA,
        ],
        compiler_params=params(),
        cost_estimate=pl.CostEstimate(flops=3 * n * rows * cols, bytes_accessed=8 * n * rows * cols, transcendentals=0),
    )(*[pltpu.with_memory_space_constraint(x, pltpu.HBM) for x in (blocks, slot)])


def store_halves(ref, index, x):
    count = x.shape[0]
    high, low = halves(x)
    ref[index, pl.ds(0, count)] = high
    ref[index, pl.ds(count, count)] = low


def product(pair, high, low, dims, low_dims):
    count = pair.shape[0] // 2
    first = lax.dot_general(pair, high, dims, preferred_element_type=jnp.float32)
    second = lax.dot_general(pair[:count], low, low_dims, preferred_element_type=jnp.float32)
    return first[:count] + first[count:] + second


def rows_kernel(steps, slot_ref, high_ref, low_ref, *refs):
    pieces, out_ref, pair_ref = refs[:-2], refs[-2], refs[-1]
    nblk, edge = high_ref.shape[0], high_ref.shape[1]
    per_piece = pieces[0].shape[1] // edge
    column_count = per_piece * len(pieces)
    me = lax.axis_index(GROUP)
    for k, piece in zip(steps, pieces):
        for h in range(per_piece):
            store_halves(pair_ref, (me ^ k) * per_piece + h, piece[:, h * edge:(h + 1) * edge])
    out_ref[...] = jnp.zeros_like(out_ref)
    for b in range(nblk):
        slot = slot_ref[b]
        r, c = lax.div(slot, column_count), lax.rem(slot, column_count)
        out_ref[r] += product(pair_ref[c], high_ref[b], low_ref[b], NN, NT)


def rows_product(slot, high, low, pieces, steps):
    count = pieces[0].shape[0]
    nblk, edge = high.shape[0], high.shape[1]
    column_count = len(pieces) * pieces[0].shape[1] // edge
    return pl.pallas_call(
        lambda *refs: rows_kernel(steps, *refs),
        out_shape=jax.ShapeDtypeStruct((RBL, count, edge), jnp.float32),
        in_specs=[smem()] + [vmem()] * (2 + len(pieces)),
        out_specs=vmem(),
        scratch_shapes=[pltpu.VMEM((column_count, 2 * count, edge), jnp.bfloat16)],
        compiler_params=params(),
    )(slot, high, low, *pieces)


def cols_kernel(column_count, slot_ref, high_ref, low_ref, *refs):
    pieces, out_ref, pair_ref = refs[:-2], refs[-2], refs[-1]
    nblk = high_ref.shape[0]
    for r in range(RBL):
        total = pieces[0][r]
        for piece in pieces[1:]:
            total = total + piece[r]
        store_halves(pair_ref, r, total)
    out_ref[...] = jnp.zeros_like(out_ref)
    for b in range(nblk):
        slot = slot_ref[b]
        r, c = lax.div(slot, column_count), lax.rem(slot, column_count)
        out_ref[c] += product(pair_ref[r], high_ref[b], low_ref[b], NN, NN)


def cols_product(slot, high, low, pieces, column_count):
    _, count, edge = pieces[0].shape
    return pl.pallas_call(
        lambda *refs: cols_kernel(column_count, *refs),
        out_shape=jax.ShapeDtypeStruct((column_count, count, edge), jnp.float32),
        in_specs=[smem()] + [vmem()] * (2 + len(pieces)),
        out_specs=vmem(),
        scratch_shapes=[pltpu.VMEM((RBL, 2 * count, edge), jnp.bfloat16)],
        compiler_params=params(),
    )(slot, high, low, *pieces)


def gram_kernel(lead, a_ref, b_ref, mine_ref, other_ref, gram_ref, z_ref):
    leads = True if lead is None else lax.axis_index("sub") == lead

    @pl.when(leads)
    def _():
        total = None
        for c in range(a_ref.shape[0]):
            z = a_ref[c] + b_ref[c]
            z_ref[c] = z
            g = lax.dot_general(z, z, NT, precision=lax.Precision.HIGHEST, preferred_element_type=jnp.float32)
            total = g if total is None else total + g
        gram_ref[...] = total
        me = lax.axis_index(GROUP)
        count = mine_ref.shape[0]
        for h in range(count):
            mine_ref[h] = z_ref[me * count + h]
            other_ref[h] = z_ref[(me ^ 1) * count + h]

    @pl.when(jnp.logical_not(leads))
    def _():
        gram_ref[...] = jnp.zeros_like(gram_ref)
        mine_ref[...] = jnp.zeros_like(mine_ref)
        other_ref[...] = jnp.zeros_like(other_ref)


def gram_of(a, b, per_share, lead):
    _, count, edge = a.shape
    share = jax.ShapeDtypeStruct((per_share, count, edge), jnp.float32)
    return pl.pallas_call(
        lambda *refs: gram_kernel(lead, *refs),
        out_shape=(share, share, jax.ShapeDtypeStruct((count, count), jnp.float32)),
        in_specs=[vmem(), vmem()],
        out_specs=(vmem(), vmem(), vmem()),
        scratch_shapes=[pltpu.VMEM(a.shape, jnp.float32)],
        compiler_params=params(),
    )(a, b)


def eliminate(g, z, scale):
    count, edge = g.shape[0], z[0].shape[1]
    row_id = lax.broadcasted_iota(jnp.int32, (count, LANES), 0)
    lane_id = lax.broadcasted_iota(jnp.int32, (count, LANES), 1)
    columns = [jnp.broadcast_to(g[:, k:k + 1], (count, LANES)) for k in range(count)]
    lower = jnp.zeros((count, LANES), jnp.float32)
    scales = jnp.zeros((count, LANES), jnp.float32)
    for j in range(count):
        column = columns[j]
        root = lax.rsqrt(column[j:j + 1, :])
        inverse = root * root
        lower = jnp.where((lane_id == j) & (row_id >= j), column * root, lower)
        scales = jnp.where(row_id == j, root, scales)
        below = jnp.where(row_id > j, column, 0.0)
        for k in range(j + 1, count):
            columns[k] = columns[k] - below * (column[k:k + 1, :] * inverse)
        if j + 1 < count:
            wide = jnp.concatenate([below] * (edge // LANES), 1)
            wide_inverse = jnp.concatenate([inverse] * (edge // LANES), 1)
            z = [x - wide * (x[j:j + 1, :] * wide_inverse) for x in z]
    scales = jnp.concatenate([scales * scale] * (edge // LANES), 1)
    return lower[:, :count].T, [x * scales for x in z]


def solve_kernel(scale, lead, z_ref, far_z_ref, *refs):
    grams, mine_ref, other_ref = refs[:-2], refs[-2], refs[-1]
    leads = True if lead is None else lax.axis_index("sub") == lead
    per_share, count, edge = z_ref.shape

    @pl.when(leads)
    def _():
        g = grams[0][...]
        for ref in grams[1:]:
            g = g + ref[...]
        factor, z = eliminate(g, [ref[h] for ref in (z_ref, far_z_ref) for h in range(per_share)], scale)
        for h in range(per_share):
            mine_ref[:, h * edge:(h + 1) * edge] = z[h]
            other_ref[:, h * edge:(h + 1) * edge] = z[per_share + h]
        other_ref[:, per_share * edge:] = jnp.zeros((count, LANES), jnp.float32)
        other_ref[:, per_share * edge:per_share * edge + count] = factor

    @pl.when(jnp.logical_not(leads))
    def _():
        mine_ref[...] = jnp.zeros_like(mine_ref)
        other_ref[...] = jnp.zeros_like(other_ref)


def solve(scale, lead, z, far_z, grams):
    per_share, count, edge = z.shape
    share = per_share * edge
    return pl.pallas_call(
        lambda *refs: solve_kernel(scale, lead, *refs),
        out_shape=(
            jax.ShapeDtypeStruct((count, share), jnp.float32),
            jax.ShapeDtypeStruct((count, share + LANES), jnp.float32),
        ),
        in_specs=[vmem()] * (2 + len(grams)),
        out_specs=(vmem(), vmem()),
        compiler_params=params(),
    )(z, far_z, *grams)


def pick_kernel(mine_ref, other_ref, far_ref, out_ref, factor_ref):
    leads = lax.axis_index("sub") == LEAD
    share, count = out_ref.shape[1], factor_ref.shape[0]
    out_ref[...] = jnp.where(leads, mine_ref[...], far_ref[:, :share])
    factor_ref[...] = jnp.where(leads, other_ref[:, share:share + count], far_ref[:, share:share + count])


def pick(mine, other, far):
    count, share = mine.shape
    return pl.pallas_call(
        pick_kernel,
        out_shape=(
            jax.ShapeDtypeStruct((count, share), jnp.float32),
            jax.ShapeDtypeStruct((count, count), jnp.float32),
        ),
        in_specs=[vmem()] * 3,
        out_specs=(vmem(), vmem()),
        compiler_params=params(),
    )(mine, other, far)


def partner(x, axes, k):
    n = lax.axis_size(axes)
    return lax.ppermute(x, axes, [(i, i ^ k) for i in range(n)])


def is_power(n):
    return n & (n - 1) == 0


def gather(x, axes, steps):
    return [x] + [partner(x, axes, k) for k in steps]


def exchange(x, steps):
    cols, rows, subs = (lax.axis_size(a) for a in ("col", "row", "sub"))
    place = lambda c, r, s: (c * rows + r) * subs + s
    pairs = [
        (place(c, r, s), place(steps[s][0][c], r ^ steps[s][1], s))
        for c in range(cols)
        for r in range(rows)
        for s in range(subs)
    ]
    return lax.ppermute(x, ("col", "row", "sub"), pairs)


def general(slot, high, low, ypart, column_count, per_share, scale):
    zpart = cols_product(slot, high, low, [lax.psum(ypart, "col")], column_count)
    for axis in ("sub", "row"):
        n = lax.axis_size(axis)
        if is_power(n):
            for i in range(n.bit_length() - 1):
                zpart = zpart + partner(zpart, axis, 1 << i)
        else:
            zpart = lax.psum(zpart, axis)
    z, other, gram = gram_of(zpart, jnp.zeros_like(zpart), per_share, None)
    mine, other = solve(scale, None, z, other, [lax.psum(gram, "col")])
    return mine, other[:, mine.shape[1]:mine.shape[1] + gram.shape[0]]


def four_by_two(slot, high, low, ypart, column_count, per_share, scale):
    ypieces = [ypart] + [exchange(ypart, ((COLS[a], 0), (COLS[b], 0))) for a, b in zip(*Y_ORDERS)]
    zpart = cols_product(slot, high, low, ypieces, column_count)
    zpart = zpart + partner(zpart, "sub", 1)
    z, other, gram = gram_of(zpart, exchange(zpart, ((COLS[1], 0), (COLS[0], 1))), per_share, LEAD)
    grams = [gram] + [exchange(gram, ((COLS[0], 1), (COLS[k], 0))) for k in G_ORDER]
    mine, other = solve(scale, LEAD, z, other, grams)
    return pick(mine, other, partner(other, "sub", 1))


def body(blocks, block_slot, basis_in):
    edge = blocks.shape[-1]
    nblk = blocks.shape[2]
    share = basis_in.shape[1]
    column_count = share * lax.axis_size(GROUP) // edge
    slot = block_slot.reshape(nblk)
    *split, slot = split_blocks(blocks.reshape(nblk, edge, edge), slot)
    high, low, high_t = [pltpu.with_memory_space_constraint(x, pltpu.VMEM) for x in split]
    slot = pltpu.with_memory_space_constraint(slot, pltpu.SMEM)
    steps = (3, 2, 1) if lax.axis_size(GROUP) == 4 else tuple(range(1, lax.axis_size(GROUP)))
    ypart = rows_product(slot, high_t, low, gather(basis_in, GROUP, steps), (0,) + steps)
    scale = math.sqrt(share * lax.axis_size(("col",) + GROUP))
    sizes = tuple(lax.axis_size(a) for a in ("col", "row", "sub"))
    finish = four_by_two if sizes == (4, 2, 2) else general
    return finish(slot, high, low, ypart, column_count, share // edge, scale)


def solution(mesh):
    in_specs = (
        P(("dom", "row", "sub"), "col", None, None, None),
        P(("dom", "row", "sub"), "col", None),
        P(None, ("dom", "col", "row", "sub")),
    )
    out_specs = (P(None, ("dom", "col", "row", "sub")), P("dom", None))
    return jax.shard_map(body, mesh=mesh, in_specs=in_specs, out_specs=out_specs, check_vma=False)
```

```python
import math

import jax
import jax.numpy as jnp
from jax import lax
from jax.experimental import pallas as pl
from jax.experimental.pallas import tpu as pltpu
from jax.sharding import PartitionSpec as P

RBL = 4
LANES = 128
LOW_T = 5
GROUP = ("row", "sub")
LEAD = 1
COLS = ((0, 1, 2, 3), (1, 0, 3, 2), (2, 3, 0, 1), (3, 2, 1, 0), (1, 3, 0, 2), (2, 0, 3, 1))
Y_ORDERS = ((3, 1, 2), (2, 3, 1))
G_ORDER = (4, 3, 5)
VMEM_LIMIT = 24 * 1024 * 1024

NT = (((1,), (1,)), ((), ()))
NN = (((1,), (0,)), ((), ()))


def params():
    return pltpu.CompilerParams(vmem_limit_bytes=VMEM_LIMIT)


def vmem():
    return pl.BlockSpec(memory_space=pltpu.VMEM)


def smem():
    return pl.BlockSpec(memory_space=pltpu.SMEM)


def halves(x):
    high = x.astype(jnp.bfloat16)
    low = (x - high.astype(jnp.float32)).astype(jnp.bfloat16)
    return high, low


def split_kernel(blocks_ref, slot_ref, high_ref, low_ref, high_t_ref, low_t_ref, place_ref, held_ref, sems, slot_sem):
    count = blocks_ref.shape[0]
    place = pltpu.make_async_copy(slot_ref, place_ref, slot_sem)
    place.start()
    copies = [pltpu.make_async_copy(blocks_ref.at[i], held_ref.at[i], sems.at[i]) for i in range(count)]
    for copy in copies:
        copy.start()
    for i, copy in enumerate(copies):
        copy.wait()
        high, low = halves(held_ref[i])
        high_ref[i], low_ref[i] = high, low
        high_t_ref[i] = high.T
        if i < LOW_T:
            low_t_ref[i] = low.T
    place.wait()


def split_blocks(blocks, slot):
    n, rows, cols = blocks.shape
    return pl.pallas_call(
        split_kernel,
        out_shape=(
            pltpu.VMEM(blocks.shape, jnp.bfloat16),
            pltpu.VMEM(blocks.shape, jnp.bfloat16),
            pltpu.VMEM(blocks.shape, jnp.bfloat16),
            pltpu.VMEM((LOW_T, cols, rows), jnp.bfloat16),
            pltpu.SMEM(slot.shape, jnp.int32),
        ),
        in_specs=[pl.BlockSpec(memory_space=pltpu.HBM)] * 2,
        out_specs=(vmem(), vmem(), vmem(), vmem(), smem()),
        scratch_shapes=[
            pltpu.VMEM(blocks.shape, jnp.float32),
            pltpu.SemaphoreType.DMA((n,)),
            pltpu.SemaphoreType.DMA,
        ],
        compiler_params=params(),
        cost_estimate=pl.CostEstimate(flops=3 * n * rows * cols, bytes_accessed=8 * n * rows * cols, transcendentals=0),
    )(*[pltpu.with_memory_space_constraint(x, pltpu.HBM) for x in (blocks, slot)])


def store_halves(ref, index, x):
    count = x.shape[0]
    high, low = halves(x)
    ref[index, pl.ds(0, count)] = high
    ref[index, pl.ds(count, count)] = low


def product(pair, high, low, dims, low_dims):
    count = pair.shape[0] // 2
    first = lax.dot_general(pair, high, dims, preferred_element_type=jnp.float32)
    second = lax.dot_general(pair[:count], low, low_dims, preferred_element_type=jnp.float32)
    return first[:count] + first[count:] + second


def rows_kernel(steps, slot_ref, high_ref, low_ref, low_t_ref, *refs):
    pieces, out_ref, pair_ref = refs[:-2], refs[-2], refs[-1]
    nblk, edge = high_ref.shape[0], high_ref.shape[1]
    per_piece = pieces[0].shape[1] // edge
    column_count = per_piece * len(pieces)
    me = lax.axis_index(GROUP)
    for k, piece in zip(steps, pieces):
        for h in range(per_piece):
            store_halves(pair_ref, (me ^ k) * per_piece + h, piece[:, h * edge:(h + 1) * edge])
    out_ref[...] = jnp.zeros_like(out_ref)
    for b in range(nblk):
        slot = slot_ref[b]
        r, c = lax.div(slot, column_count), lax.rem(slot, column_count)
        out_ref[r] += product(pair_ref[c], high_ref[b], *((low_t_ref[b], NN, NN) if b < LOW_T else (low_ref[b], NN, NT)))


def rows_product(slot, high, low, low_t, pieces, steps):
    count = pieces[0].shape[0]
    nblk, edge = high.shape[0], high.shape[1]
    column_count = len(pieces) * pieces[0].shape[1] // edge
    return pl.pallas_call(
        lambda *refs: rows_kernel(steps, *refs),
        out_shape=jax.ShapeDtypeStruct((RBL, count, edge), jnp.float32),
        in_specs=[smem()] + [vmem()] * (3 + len(pieces)),
        out_specs=vmem(),
        scratch_shapes=[pltpu.VMEM((column_count, 2 * count, edge), jnp.bfloat16)],
        compiler_params=params(),
    )(slot, high, low, low_t, *pieces)


def cols_kernel(column_count, slot_ref, high_ref, low_ref, *refs):
    pieces, out_ref, pair_ref = refs[:-2], refs[-2], refs[-1]
    nblk = high_ref.shape[0]
    for r in range(RBL):
        total = pieces[0][r]
        for piece in pieces[1:]:
            total = total + piece[r]
        store_halves(pair_ref, r, total)
    out_ref[...] = jnp.zeros_like(out_ref)
    for b in range(nblk):
        slot = slot_ref[b]
        r, c = lax.div(slot, column_count), lax.rem(slot, column_count)
        out_ref[c] += product(pair_ref[r], high_ref[b], low_ref[b], NN, NN)


def cols_product(slot, high, low, pieces, column_count):
    _, count, edge = pieces[0].shape
    return pl.pallas_call(
        lambda *refs: cols_kernel(column_count, *refs),
        out_shape=jax.ShapeDtypeStruct((column_count, count, edge), jnp.float32),
        in_specs=[smem()] + [vmem()] * (2 + len(pieces)),
        out_specs=vmem(),
        scratch_shapes=[pltpu.VMEM((RBL, 2 * count, edge), jnp.bfloat16)],
        compiler_params=params(),
    )(slot, high, low, *pieces)


def gram_kernel(lead, a_ref, b_ref, mine_ref, other_ref, gram_ref, z_ref):
    leads = True if lead is None else lax.axis_index("sub") == lead

    @pl.when(leads)
    def _():
        total = None
        for c in range(a_ref.shape[0]):
            z = a_ref[c] + b_ref[c]
            z_ref[c] = z
            g = lax.dot_general(z, z, NT, precision=lax.Precision.HIGHEST, preferred_element_type=jnp.float32)
            total = g if total is None else total + g
        gram_ref[...] = total
        me = lax.axis_index(GROUP)
        count = mine_ref.shape[0]
        for h in range(count):
            mine_ref[h] = z_ref[me * count + h]
            other_ref[h] = z_ref[(me ^ 1) * count + h]

    @pl.when(jnp.logical_not(leads))
    def _():
        gram_ref[...] = jnp.zeros_like(gram_ref)
        mine_ref[...] = jnp.zeros_like(mine_ref)
        other_ref[...] = jnp.zeros_like(other_ref)


def gram_of(a, b, per_share, lead):
    _, count, edge = a.shape
    share = jax.ShapeDtypeStruct((per_share, count, edge), jnp.float32)
    return pl.pallas_call(
        lambda *refs: gram_kernel(lead, *refs),
        out_shape=(share, share, jax.ShapeDtypeStruct((count, count), jnp.float32)),
        in_specs=[vmem(), vmem()],
        out_specs=(vmem(), vmem(), vmem()),
        scratch_shapes=[pltpu.VMEM(a.shape, jnp.float32)],
        compiler_params=params(),
    )(a, b)


def eliminate(g, z, scale):
    count, edge = g.shape[0], z[0].shape[1]
    row_id = lax.broadcasted_iota(jnp.int32, (count, LANES), 0)
    lane_id = lax.broadcasted_iota(jnp.int32, (count, LANES), 1)
    columns = [jnp.broadcast_to(g[:, k:k + 1], (count, LANES)) for k in range(count)]
    lower = jnp.zeros((count, LANES), jnp.float32)
    scales = jnp.zeros((count, LANES), jnp.float32)
    for j in range(count):
        column = columns[j]
        root = lax.rsqrt(column[j:j + 1, :])
        inverse = root * root
        lower = jnp.where((lane_id == j) & (row_id >= j), column * root, lower)
        scales = jnp.where(row_id == j, root, scales)
        below = jnp.where(row_id > j, column, 0.0)
        for k in range(j + 1, count):
            columns[k] = columns[k] - below * (column[k:k + 1, :] * inverse)
        if j + 1 < count:
            wide = jnp.concatenate([below] * (edge // LANES), 1)
            wide_inverse = jnp.concatenate([inverse] * (edge // LANES), 1)
            z = [x - wide * (x[j:j + 1, :] * wide_inverse) for x in z]
    scales = jnp.concatenate([scales * scale] * (edge // LANES), 1)
    return lower[:, :count].T, [x * scales for x in z]


def solve_kernel(scale, lead, z_ref, far_z_ref, *refs):
    grams, mine_ref, other_ref = refs[:-2], refs[-2], refs[-1]
    leads = True if lead is None else lax.axis_index("sub") == lead
    per_share, count, edge = z_ref.shape

    @pl.when(leads)
    def _():
        g = grams[0][...]
        for ref in grams[1:]:
            g = g + ref[...]
        factor, z = eliminate(g, [ref[h] for ref in (z_ref, far_z_ref) for h in range(per_share)], scale)
        for h in range(per_share):
            mine_ref[:, h * edge:(h + 1) * edge] = z[h]
            other_ref[:, h * edge:(h + 1) * edge] = z[per_share + h]
        other_ref[:, per_share * edge:] = jnp.zeros((count, LANES), jnp.float32)
        other_ref[:, per_share * edge:per_share * edge + count] = factor

    @pl.when(jnp.logical_not(leads))
    def _():
        mine_ref[...] = jnp.zeros_like(mine_ref)
        other_ref[...] = jnp.zeros_like(other_ref)


def solve(scale, lead, z, far_z, grams):
    per_share, count, edge = z.shape
    share = per_share * edge
    return pl.pallas_call(
        lambda *refs: solve_kernel(scale, lead, *refs),
        out_shape=(
            jax.ShapeDtypeStruct((count, share), jnp.float32),
            jax.ShapeDtypeStruct((count, share + LANES), jnp.float32),
        ),
        in_specs=[vmem()] * (2 + len(grams)),
        out_specs=(vmem(), vmem()),
        compiler_params=params(),
    )(z, far_z, *grams)


def pick_kernel(mine_ref, other_ref, far_ref, out_ref, factor_ref):
    leads = lax.axis_index("sub") == LEAD
    share, count = out_ref.shape[1], factor_ref.shape[0]
    out_ref[...] = jnp.where(leads, mine_ref[...], far_ref[:, :share])
    factor_ref[...] = jnp.where(leads, other_ref[:, share:share + count], far_ref[:, share:share + count])


def pick(mine, other, far):
    count, share = mine.shape
    return pl.pallas_call(
        pick_kernel,
        out_shape=(
            jax.ShapeDtypeStruct((count, share), jnp.float32),
            jax.ShapeDtypeStruct((count, count), jnp.float32),
        ),
        in_specs=[vmem()] * 3,
        out_specs=(vmem(), vmem()),
        compiler_params=params(),
    )(mine, other, far)


def partner(x, axes, k):
    n = lax.axis_size(axes)
    return lax.ppermute(x, axes, [(i, i ^ k) for i in range(n)])


def is_power(n):
    return n & (n - 1) == 0


def gather(x, axes, steps):
    return [x] + [partner(x, axes, k) for k in steps]


def exchange(x, steps):
    cols, rows, subs = (lax.axis_size(a) for a in ("col", "row", "sub"))
    place = lambda c, r, s: (c * rows + r) * subs + s
    pairs = [
        (place(c, r, s), place(steps[s][0][c], r ^ steps[s][1], s))
        for c in range(cols)
        for r in range(rows)
        for s in range(subs)
    ]
    return lax.ppermute(x, ("col", "row", "sub"), pairs)


def general(slot, high, low, ypart, column_count, per_share, scale):
    zpart = cols_product(slot, high, low, [lax.psum(ypart, "col")], column_count)
    for axis in ("sub", "row"):
        n = lax.axis_size(axis)
        if is_power(n):
            for i in range(n.bit_length() - 1):
                zpart = zpart + partner(zpart, axis, 1 << i)
        else:
            zpart = lax.psum(zpart, axis)
    z, other, gram = gram_of(zpart, jnp.zeros_like(zpart), per_share, None)
    mine, other = solve(scale, None, z, other, [lax.psum(gram, "col")])
    return mine, other[:, mine.shape[1]:mine.shape[1] + gram.shape[0]]


def four_by_two(slot, high, low, ypart, column_count, per_share, scale):
    ypieces = [ypart] + [exchange(ypart, ((COLS[a], 0), (COLS[b], 0))) for a, b in zip(*Y_ORDERS)]
    zpart = cols_product(slot, high, low, ypieces, column_count)
    zpart = zpart + partner(zpart, "sub", 1)
    z, other, gram = gram_of(zpart, exchange(zpart, ((COLS[1], 0), (COLS[0], 1))), per_share, LEAD)
    grams = [gram] + [exchange(gram, ((COLS[0], 1), (COLS[k], 0))) for k in G_ORDER]
    mine, other = solve(scale, LEAD, z, other, grams)
    return pick(mine, other, partner(other, "sub", 1))


def body(blocks, block_slot, basis_in):
    edge = blocks.shape[-1]
    nblk = blocks.shape[2]
    share = basis_in.shape[1]
    column_count = share * lax.axis_size(GROUP) // edge
    slot = block_slot.reshape(nblk)
    *split, slot = split_blocks(blocks.reshape(nblk, edge, edge), slot)
    high, low, high_t, low_t = [pltpu.with_memory_space_constraint(x, pltpu.VMEM) for x in split]
    slot = pltpu.with_memory_space_constraint(slot, pltpu.SMEM)
    steps = (3, 2, 1) if lax.axis_size(GROUP) == 4 else tuple(range(1, lax.axis_size(GROUP)))
    ypart = rows_product(slot, high_t, low, low_t, gather(basis_in, GROUP, steps), (0,) + steps)
    scale = math.sqrt(share * lax.axis_size(("col",) + GROUP))
    sizes = tuple(lax.axis_size(a) for a in ("col", "row", "sub"))
    finish = four_by_two if sizes == (4, 2, 2) else general
    return finish(slot, high, low, ypart, column_count, share // edge, scale)


def solution(mesh):
    in_specs = (
        P(("dom", "row", "sub"), "col", None, None, None),
        P(("dom", "row", "sub"), "col", None),
        P(None, ("dom", "col", "row", "sub")),
    )
    out_specs = (P(None, ("dom", "col", "row", "sub")), P("dom", None))
    return jax.shard_map(body, mesh=mesh, in_specs=in_specs, out_specs=out_specs, check_vma=False)
```

```python
import math

import jax
import jax.numpy as jnp
from jax import lax
from jax.experimental import pallas as pl
from jax.experimental.pallas import tpu as pltpu
from jax.sharding import PartitionSpec as P

RBL = 4
LANES = 128
LOW_T = 5
GROUP = ("row", "sub")
LEAD = 1
COLS = ((0, 1, 2, 3), (1, 0, 3, 2), (2, 3, 0, 1), (3, 2, 1, 0), (1, 3, 0, 2), (2, 0, 3, 1))
Y_ORDERS = ((3, 1, 2), (2, 3, 1))
G_ORDER = (4, 3, 5)
VMEM_LIMIT = 24 * 1024 * 1024

NT = (((1,), (1,)), ((), ()))
NN = (((1,), (0,)), ((), ()))


def params():
    return pltpu.CompilerParams(vmem_limit_bytes=VMEM_LIMIT)


def vmem():
    return pl.BlockSpec(memory_space=pltpu.VMEM)


def smem():
    return pl.BlockSpec(memory_space=pltpu.SMEM)


def halves(x):
    high = x.astype(jnp.bfloat16)
    low = (x - high.astype(jnp.float32)).astype(jnp.bfloat16)
    return high, low


def split_kernel(blocks_ref, slot_ref, high_ref, low_ref, high_t_ref, low_t_ref, place_ref, held_ref, sems, slot_sem):
    count = blocks_ref.shape[0]
    place = pltpu.make_async_copy(slot_ref, place_ref, slot_sem)
    place.start()
    copies = [pltpu.make_async_copy(blocks_ref.at[i], held_ref.at[i], sems.at[i]) for i in range(count)]
    for copy in copies:
        copy.start()
    for i, copy in enumerate(copies):
        copy.wait()
        high, low = halves(held_ref[i])
        high_ref[i], low_ref[i] = high, low
        high_t_ref[i] = high.T
        if i < LOW_T:
            low_t_ref[i] = low.T
    place.wait()


def split_blocks(blocks, slot):
    n, rows, cols = blocks.shape
    return pl.pallas_call(
        split_kernel,
        out_shape=(
            pltpu.VMEM(blocks.shape, jnp.bfloat16),
            pltpu.VMEM(blocks.shape, jnp.bfloat16),
            pltpu.VMEM(blocks.shape, jnp.bfloat16),
            pltpu.VMEM((LOW_T, cols, rows), jnp.bfloat16),
            pltpu.SMEM(slot.shape, jnp.int32),
        ),
        in_specs=[pl.BlockSpec(memory_space=pltpu.HBM)] * 2,
        out_specs=(vmem(), vmem(), vmem(), vmem(), smem()),
        scratch_shapes=[
            pltpu.VMEM(blocks.shape, jnp.float32),
            pltpu.SemaphoreType.DMA((n,)),
            pltpu.SemaphoreType.DMA,
        ],
        compiler_params=params(),
        cost_estimate=pl.CostEstimate(flops=3 * n * rows * cols, bytes_accessed=8 * n * rows * cols, transcendentals=0),
    )(*[pltpu.with_memory_space_constraint(x, pltpu.HBM) for x in (blocks, slot)])


def store_halves(ref, index, x):
    count = x.shape[0]
    high, low = halves(x)
    ref[index, pl.ds(0, count)] = high
    ref[index, pl.ds(count, count)] = low


def product(pair, high, low, dims, low_dims):
    count = pair.shape[0] // 2
    first = lax.dot_general(pair, high, dims, preferred_element_type=jnp.float32)
    second = lax.dot_general(pair[:count], low, low_dims, preferred_element_type=jnp.float32)
    return first[:count] + first[count:] + second


def rows_kernel(steps, slot_ref, high_ref, low_ref, low_t_ref, *refs):
    pieces, out_ref, pair_ref = refs[:-2], refs[-2], refs[-1]
    nblk, edge = high_ref.shape[0], high_ref.shape[1]
    per_piece = pieces[0].shape[1] // edge
    column_count = per_piece * len(pieces)
    me = lax.axis_index(GROUP)
    for k, piece in zip(steps, pieces):
        for h in range(per_piece):
            store_halves(pair_ref, (me ^ k) * per_piece + h, piece[:, h * edge:(h + 1) * edge])
    out_ref[...] = jnp.zeros_like(out_ref)
    for b in range(nblk):
        slot = slot_ref[b]
        r, c = lax.div(slot, column_count), lax.rem(slot, column_count)
        out_ref[r] += product(pair_ref[c], high_ref[b], *((low_t_ref[b], NN, NN) if b < LOW_T else (low_ref[b], NN, NT)))


def rows_product(slot, high, low, low_t, pieces, steps):
    count = pieces[0].shape[0]
    nblk, edge = high.shape[0], high.shape[1]
    column_count = len(pieces) * pieces[0].shape[1] // edge
    return pl.pallas_call(
        lambda *refs: rows_kernel(steps, *refs),
        out_shape=jax.ShapeDtypeStruct((RBL, count, edge), jnp.float32),
        in_specs=[smem()] + [vmem()] * (3 + len(pieces)),
        out_specs=vmem(),
        scratch_shapes=[pltpu.VMEM((column_count, 2 * count, edge), jnp.bfloat16)],
        compiler_params=params(),
    )(slot, high, low, low_t, *pieces)


def cols_kernel(column_count, slot_ref, high_ref, low_ref, *refs):
    pieces, out_ref, pair_ref = refs[:-2], refs[-2], refs[-1]
    nblk = high_ref.shape[0]
    for r in range(RBL):
        total = pieces[0][r]
        for piece in pieces[1:]:
            total = total + piece[r]
        store_halves(pair_ref, r, total)
    out_ref[...] = jnp.zeros_like(out_ref)
    for b in range(nblk):
        slot = slot_ref[b]
        r, c = lax.div(slot, column_count), lax.rem(slot, column_count)
        out_ref[c] += product(pair_ref[r], high_ref[b], low_ref[b], NN, NN)


def cols_product(slot, high, low, pieces, column_count):
    _, count, edge = pieces[0].shape
    return pl.pallas_call(
        lambda *refs: cols_kernel(column_count, *refs),
        out_shape=jax.ShapeDtypeStruct((column_count, count, edge), jnp.float32),
        in_specs=[smem()] + [vmem()] * (2 + len(pieces)),
        out_specs=vmem(),
        scratch_shapes=[pltpu.VMEM((RBL, 2 * count, edge), jnp.bfloat16)],
        compiler_params=params(),
    )(slot, high, low, *pieces)


def gram_kernel(lead, a_ref, b_ref, mine_ref, other_ref, gram_ref, z_ref):
    leads = True if lead is None else lax.axis_index("sub") == lead

    @pl.when(leads)
    def _():
        total = None
        for c in range(a_ref.shape[0]):
            z = a_ref[c] + b_ref[c]
            z_ref[c] = z
            both = jnp.concatenate(halves(z), axis=0)
            g = lax.dot_general(both, both, NT, preferred_element_type=jnp.float32)
            total = g if total is None else total + g
        n = gram_ref.shape[0]
        gram_ref[...] = total[:n, :n] + total[:n, n:] + total[n:, :n] + total[n:, n:]
        me = lax.axis_index(GROUP)
        count = mine_ref.shape[0]
        for h in range(count):
            mine_ref[h] = z_ref[me * count + h]
            other_ref[h] = z_ref[(me ^ 1) * count + h]

    @pl.when(jnp.logical_not(leads))
    def _():
        gram_ref[...] = jnp.zeros_like(gram_ref)
        mine_ref[...] = jnp.zeros_like(mine_ref)
        other_ref[...] = jnp.zeros_like(other_ref)


def gram_of(a, b, per_share, lead):
    _, count, edge = a.shape
    share = jax.ShapeDtypeStruct((per_share, count, edge), jnp.float32)
    return pl.pallas_call(
        lambda *refs: gram_kernel(lead, *refs),
        out_shape=(share, share, jax.ShapeDtypeStruct((count, count), jnp.float32)),
        in_specs=[vmem(), vmem()],
        out_specs=(vmem(), vmem(), vmem()),
        scratch_shapes=[pltpu.VMEM(a.shape, jnp.float32)],
        compiler_params=params(),
    )(a, b)


def eliminate(g, z, scale):
    count, edge = g.shape[0], z[0].shape[1]
    row_id = lax.broadcasted_iota(jnp.int32, (count, LANES), 0)
    lane_id = lax.broadcasted_iota(jnp.int32, (count, LANES), 1)
    columns = [jnp.broadcast_to(g[:, k:k + 1], (count, LANES)) for k in range(count)]
    lower = jnp.zeros((count, LANES), jnp.float32)
    scales = jnp.zeros((count, LANES), jnp.float32)
    for j in range(count):
        column = columns[j]
        root = lax.rsqrt(column[j:j + 1, :])
        inverse = root * root
        lower = jnp.where((lane_id == j) & (row_id >= j), column * root, lower)
        scales = jnp.where(row_id == j, root, scales)
        below = jnp.where(row_id > j, column, 0.0)
        for k in range(j + 1, count):
            columns[k] = columns[k] - below * (column[k:k + 1, :] * inverse)
        if j + 1 < count:
            wide = jnp.concatenate([below] * (edge // LANES), 1)
            wide_inverse = jnp.concatenate([inverse] * (edge // LANES), 1)
            z = [x - wide * (x[j:j + 1, :] * wide_inverse) for x in z]
    scales = jnp.concatenate([scales * scale] * (edge // LANES), 1)
    return lower[:, :count].T, [x * scales for x in z]


def solve_kernel(scale, lead, z_ref, far_z_ref, *refs):
    grams, mine_ref, other_ref = refs[:-2], refs[-2], refs[-1]
    leads = True if lead is None else lax.axis_index("sub") == lead
    per_share, count, edge = z_ref.shape

    @pl.when(leads)
    def _():
        g = grams[0][...]
        for ref in grams[1:]:
            g = g + ref[...]
        factor, z = eliminate(g, [ref[h] for ref in (z_ref, far_z_ref) for h in range(per_share)], scale)
        for h in range(per_share):
            mine_ref[:, h * edge:(h + 1) * edge] = z[h]
            other_ref[:, h * edge:(h + 1) * edge] = z[per_share + h]
        other_ref[:, per_share * edge:] = jnp.zeros((count, LANES), jnp.float32)
        other_ref[:, per_share * edge:per_share * edge + count] = factor

    @pl.when(jnp.logical_not(leads))
    def _():
        mine_ref[...] = jnp.zeros_like(mine_ref)
        other_ref[...] = jnp.zeros_like(other_ref)


def solve(scale, lead, z, far_z, grams):
    per_share, count, edge = z.shape
    share = per_share * edge
    return pl.pallas_call(
        lambda *refs: solve_kernel(scale, lead, *refs),
        out_shape=(
            jax.ShapeDtypeStruct((count, share), jnp.float32),
            jax.ShapeDtypeStruct((count, share + LANES), jnp.float32),
        ),
        in_specs=[vmem()] * (2 + len(grams)),
        out_specs=(vmem(), vmem()),
        compiler_params=params(),
    )(z, far_z, *grams)


def pick_kernel(mine_ref, other_ref, far_ref, out_ref, factor_ref):
    leads = lax.axis_index("sub") == LEAD
    share, count = out_ref.shape[1], factor_ref.shape[0]
    out_ref[...] = jnp.where(leads, mine_ref[...], far_ref[:, :share])
    factor_ref[...] = jnp.where(leads, other_ref[:, share:share + count], far_ref[:, share:share + count])


def pick(mine, other, far):
    count, share = mine.shape
    return pl.pallas_call(
        pick_kernel,
        out_shape=(
            jax.ShapeDtypeStruct((count, share), jnp.float32),
            jax.ShapeDtypeStruct((count, count), jnp.float32),
        ),
        in_specs=[vmem()] * 3,
        out_specs=(vmem(), vmem()),
        compiler_params=params(),
    )(mine, other, far)


def partner(x, axes, k):
    n = lax.axis_size(axes)
    return lax.ppermute(x, axes, [(i, i ^ k) for i in range(n)])


def is_power(n):
    return n & (n - 1) == 0


def gather(x, axes, steps):
    return [x] + [partner(x, axes, k) for k in steps]


def exchange(x, steps):
    cols, rows, subs = (lax.axis_size(a) for a in ("col", "row", "sub"))
    place = lambda c, r, s: (c * rows + r) * subs + s
    pairs = [
        (place(c, r, s), place(steps[s][0][c], r ^ steps[s][1], s))
        for c in range(cols)
        for r in range(rows)
        for s in range(subs)
    ]
    return lax.ppermute(x, ("col", "row", "sub"), pairs)


def general(slot, high, low, ypart, column_count, per_share, scale):
    zpart = cols_product(slot, high, low, [lax.psum(ypart, "col")], column_count)
    for axis in ("sub", "row"):
        n = lax.axis_size(axis)
        if is_power(n):
            for i in range(n.bit_length() - 1):
                zpart = zpart + partner(zpart, axis, 1 << i)
        else:
            zpart = lax.psum(zpart, axis)
    z, other, gram = gram_of(zpart, jnp.zeros_like(zpart), per_share, None)
    mine, other = solve(scale, None, z, other, [lax.psum(gram, "col")])
    return mine, other[:, mine.shape[1]:mine.shape[1] + gram.shape[0]]


def four_by_two(slot, high, low, ypart, column_count, per_share, scale):
    ypieces = [ypart] + [exchange(ypart, ((COLS[a], 0), (COLS[b], 0))) for a, b in zip(*Y_ORDERS)]
    zpart = cols_product(slot, high, low, ypieces, column_count)
    zpart = zpart + partner(zpart, "sub", 1)
    z, other, gram = gram_of(zpart, exchange(zpart, ((COLS[1], 0), (COLS[0], 1))), per_share, LEAD)
    grams = [gram] + [exchange(gram, ((COLS[0], 1), (COLS[k], 0))) for k in G_ORDER]
    mine, other = solve(scale, LEAD, z, other, grams)
    return pick(mine, other, partner(other, "sub", 1))


def body(blocks, block_slot, basis_in):
    edge = blocks.shape[-1]
    nblk = blocks.shape[2]
    share = basis_in.shape[1]
    column_count = share * lax.axis_size(GROUP) // edge
    slot = block_slot.reshape(nblk)
    *split, slot = split_blocks(blocks.reshape(nblk, edge, edge), slot)
    high, low, high_t, low_t = [pltpu.with_memory_space_constraint(x, pltpu.VMEM) for x in split]
    slot = pltpu.with_memory_space_constraint(slot, pltpu.SMEM)
    steps = (3, 2, 1) if lax.axis_size(GROUP) == 4 else tuple(range(1, lax.axis_size(GROUP)))
    ypart = rows_product(slot, high_t, low, low_t, gather(basis_in, GROUP, steps), (0,) + steps)
    scale = math.sqrt(share * lax.axis_size(("col",) + GROUP))
    sizes = tuple(lax.axis_size(a) for a in ("col", "row", "sub"))
    finish = four_by_two if sizes == (4, 2, 2) else general
    return finish(slot, high, low, ypart, column_count, share // edge, scale)


def solution(mesh):
    in_specs = (
        P(("dom", "row", "sub"), "col", None, None, None),
        P(("dom", "row", "sub"), "col", None),
        P(None, ("dom", "col", "row", "sub")),
    )
    out_specs = (P(None, ("dom", "col", "row", "sub")), P("dom", None))
    return jax.shard_map(body, mesh=mesh, in_specs=in_specs, out_specs=out_specs, check_vma=False)
```
